32 devices in a mesh: req: 8 (over y, x, core), tp: 4 (over z).
Axes of the slice: x: 2, y: 2, z: 4, core: 2. Of those that a mesh axis runs over, the one named last changes fastest.
Arguments:
- hidden: bfloat16 [64, 24, 2560], P('req', None, 'tp'), may hold values from -6 to 6
- norm_gain: float32 [2560], replicated, may hold values from 0.25 to 1.75
- w_query: bfloat16 [2560, 2560], P(None, 'tp'), may hold values from -0.125 to 0.125
- w_keyval: bfloat16 [1280, 2560], P('tp'), may hold values from -0.125 to 0.125
- w_out: bfloat16 [2560, 2560], P('tp'), may hold values from -0.25 to 0.25
- kv_cache: bfloat16 [64, 1280, 512], P('req', 'tp'), as said below
- lengths: int32 [64], P('req'), may hold values from 2 to 508, as said below
- parents: int32 [64, 24], P('req'), may hold values from 0 to 22, as said below
- accepted: int32 [64, 4], P('req'), may hold values from 0 to 6, as said below
- slot_of: int32 [64], P('req'), may hold values from 0 to 63, as said below
Outputs:
- out_rows: bfloat16 [64, 24, 2560], P('req', None, 'tp')
- new_cache: bfloat16 [64, 1280, 512], P('req', 'tp')
The draws below stay inside these ranges and needn't reach their ends.
Inputs may be any that keep to these rules, and one draw needn't show every extreme that they name: `lengths`: some request has exactly 508 cached tokens. parents[r, 0] = 0 and parents[r, t] is t - 1 or max(t - 2, 0) for t >= 1. accepted[r, m] is the tree token at depth m on the path from token 0 to one token of request r, so accepted[r, 0] = 0. A permutation; the 8 requests held by req index i go to 8 different req indices, one to each: a request of index i lands in slot d * 8 + i, where d = slot_of // 8. `kv_cache`: keys and values of cached tokens; positions at or past a request's length are not read.
All inputs are finite; a program needn't handle non-finite values.
Results may differ from the reference program's by a relative error of at most 0.012.
Values may be sent and summed in bfloat16 or wider, within the bound.
A program may use at most 128 MiB of HBM per device.

```python
import math
import jax
import jax.numpy as jnp
from jax import lax

D = 2560
H = 32
KVH = 8
HD = 80
TREE = 24
CACHE = 512
DEPTH = 4
REQ_DEV = 8
REQS = 64
N_REQ = 8
N_TP = 4


def length_values(key):
    top_length = CACHE - DEPTH
    source = jnp.arange(REQS, dtype=jnp.int32) // REQ_DEV
    ceiling = 2 + (top_length - 2) * (1 + source % 4) // 4
    drawn = jax.random.randint(jax.random.fold_in(key, 11), (REQS,), 2, ceiling + 1)
    chosen = jax.random.randint(jax.random.fold_in(key, 12), (), 0, REQS)
    return jnp.where(jnp.arange(REQS, dtype=jnp.int32) == chosen, top_length, drawn).astype(jnp.int32)


def tree_parents(key):
    steps_back = jax.random.randint(jax.random.fold_in(key, 21), (REQS, TREE), 1, 3)
    first_last = jnp.logical_and(jnp.arange(REQS, dtype=jnp.int32)[:, None] == 0, jnp.arange(TREE, dtype=jnp.int32)[None, :] == TREE - 1)
    steps_back = jnp.where(first_last, 1, steps_back)
    return jnp.maximum(jnp.arange(TREE, dtype=jnp.int32)[None, :] - steps_back, 0).astype(jnp.int32)


def draw_lengths(key, part):
    return length_values(key)


def draw_parents(key, part):
    return tree_parents(key)


def draw_accepted(key, part):
    parents = tree_parents(key)
    end_token = (TREE - 1 - jax.random.randint(jax.random.fold_in(key, 22), (REQS,), 0, 2)).astype(jnp.int32)

    def climb_up(index_step, state):
        ancestor_chain, current = state
        ancestor_chain = ancestor_chain.at[:, index_step].set(current)
        current = jnp.take_along_axis(parents, current[:, None], axis=1)[:, 0]
        return (ancestor_chain, current)
    ancestor_chain, finished = lax.fori_loop(0, TREE, climb_up, (jnp.zeros((REQS, TREE), jnp.int32), end_token))
    depths = jnp.sum((ancestor_chain != 0).astype(jnp.int32), axis=1)
    levels = jnp.arange(DEPTH, dtype=jnp.int32)
    return jnp.take_along_axis(ancestor_chain, depths[:, None] - levels[None, :], axis=1).astype(jnp.int32)


def draw_slot_of(key, part):
    length_grid = length_values(key).reshape(N_REQ, REQ_DEV)
    local_index = jnp.arange(REQ_DEV, dtype=jnp.int32)
    ordering = length_grid * REQ_DEV + local_index[None, :]
    ranking = jnp.argsort(jnp.argsort(-ordering, axis=1, stable=True), axis=1, stable=True).astype(jnp.int32)
    offset = jax.random.randint(jax.random.fold_in(key, 13), (N_REQ, 1), 0, N_REQ)
    target = (ranking + offset) % N_REQ
    source_index = jnp.arange(N_REQ, dtype=jnp.int32)[:, None]
    return (target * REQ_DEV + source_index).reshape(REQS).astype(jnp.int32)


def draw_kv_cache(key, part):
    lane_count = KVH * 2 * HD
    drawn = jnp.clip(jax.random.normal(jax.random.fold_in(key, 33), (REQS, lane_count, CACHE), jnp.float32), -6.0, 6.0)
    return drawn.astype(jnp.bfloat16)


def shard_levels(own_key, extent, cuts, smallest, high):
    gain = 1.0
    for position, parts in cuts:
        steps = jax.random.uniform(jax.random.fold_in(jax.random.fold_in(own_key, 6), position), (parts,), jnp.float32, smallest / len(cuts), high / len(cuts))
        gain = gain * jnp.repeat(jnp.exp(steps), extent[position] // parts).reshape((-1,) + (1,) * (len(extent) - 1 - position))
    return gain


def bell_draw(own_key, extent, width, reach, shards=(), kind=jnp.bfloat16):
    gain = shard_levels(own_key, extent, shards, -0.22, 0.18) if shards else 1.0
    entries = jax.random.normal(own_key, extent, jnp.float32) * width * gain
    return jnp.minimum(jnp.maximum(entries, -reach), reach).astype(kind)


def setup_inputs(seed: int = 0) -> dict:
    seeds = jax.random.split(jax.random.key(seed), 11)
    return {
        "hidden": bell_draw(seeds[0], (REQS, TREE, D), 1.0, 6.0, ((0, 8), (2, 4))),
        "norm_gain": jnp.clip(1.0 + 0.15 * jax.random.normal(seeds[1], (D,), jnp.float32), 0.25, 1.75),
        "w_query": bell_draw(seeds[2], (D, H * HD), D ** -0.5, 0.125, ((1, 4),)),
        "w_keyval": bell_draw(seeds[3], (KVH * 2 * HD, D), D ** -0.5, 0.125, ((0, 4),)),
        "w_out": bell_draw(seeds[4], (H * HD, D), (H * HD // 4) ** -0.5, 0.25, ((0, 4),)),
        "kv_cache": draw_kv_cache(jax.random.fold_in(seeds[10], 71), 0),
        "lengths": draw_lengths(jax.random.fold_in(seeds[10], 71), 0),
        "parents": draw_parents(jax.random.fold_in(seeds[10], 71), 0),
        "accepted": draw_accepted(jax.random.fold_in(seeds[10], 71), 0),
        "slot_of": draw_slot_of(jax.random.fold_in(seeds[10], 71), 0),
    }


def ancestry(parents):
    tree_size = parents.shape[-1]
    tokens = jnp.arange(tree_size, dtype=jnp.int32)

    def follow(index_step, state):
        marks, depths, current = state
        marks = jnp.logical_or(marks, current[..., :, None] == tokens)
        depths = depths + (current != 0).astype(jnp.int32)
        current = jnp.take_along_axis(parents, current, axis=-1)
        return (marks, depths, current)
    start = jnp.broadcast_to(tokens, parents.shape)
    marks = jnp.zeros(parents.shape + (tree_size,), jnp.bool_)
    marks, depths, finished = lax.fori_loop(0, tree_size, follow, (marks, jnp.zeros(parents.shape, jnp.int32), start))
    return (marks, depths)

def rope_tables(positions):
    frequency = 10000.0 ** (-2.0 * jnp.arange(HD // 2, dtype=jnp.float32) / HD)
    angles = positions.astype(jnp.float32)[..., None] * frequency
    return (jnp.cos(angles), jnp.sin(angles))

def rotate_pairs(values, cosines, sines):
    half_size = values.shape[-1] // 2
    first_half = values[..., :half_size]
    second_half = values[..., half_size:]
    return jnp.concatenate([first_half * cosines - second_half * sines, second_half * cosines + first_half * sines], axis=-1)

def place_columns(kept_rows, new_columns, start):
    return lax.dynamic_update_slice(kept_rows, new_columns, (jnp.zeros((), jnp.int32), start.astype(jnp.int32)))

def reference(hidden, norm_gain, w_query, w_keyval, w_out, kv_cache, lengths, parents, accepted, slot_of):
    requests, tree_size, full_width = hidden.shape
    cache_len = kv_cache.shape[2]
    group_size = H // KVH
    score_scale = 1.0 / math.sqrt(HD)
    values = hidden.astype(jnp.float32)
    spread = lax.optimization_barrier(jnp.mean(values * values, axis=-1, keepdims=True))
    normed = (values * lax.rsqrt(spread + 1e-05) * norm_gain).astype(jnp.bfloat16)
    flat_rows = normed.reshape(requests * tree_size, full_width)
    query = jnp.dot(flat_rows, w_query, preferred_element_type=jnp.float32).reshape(requests, tree_size, KVH, group_size, HD)
    keyval = lax.dot_general(flat_rows, w_keyval, (((1,), (1,)), ((), ())), preferred_element_type=jnp.float32).reshape(requests, tree_size, KVH, 2, HD)
    ancestors, depths = ancestry(parents)
    cosines, sines = rope_tables(lengths[:, None] + depths)
    query = rotate_pairs(query, cosines[:, :, None, None], sines[:, :, None, None]).astype(jnp.bfloat16)
    keys = rotate_pairs(keyval[:, :, :, 0], cosines[:, :, None], sines[:, :, None]).astype(jnp.bfloat16)
    tree_values = keyval[:, :, :, 1].astype(jnp.bfloat16)
    tree_kv = jnp.stack([keys, tree_values], axis=3).reshape(requests, tree_size, KVH * 2 * HD)
    positions = jnp.arange(cache_len, dtype=jnp.int32)

    def attend(pieces):
        query_one, kv_one, cache_one, length_one, marks_one = pieces
        cache_rows = jnp.transpose(cache_one, (1, 0))
        joined = jnp.concatenate([cache_rows, kv_one], axis=0).reshape(cache_len + tree_size, KVH, 2, HD).astype(jnp.float32)
        live_cache = jnp.broadcast_to(positions < length_one, (tree_size, cache_len))
        live = jnp.concatenate([live_cache, marks_one], axis=1)
        scores = jnp.einsum('tgqe,cge->gqtc', query_one.astype(jnp.float32), joined[:, :, 0]) * score_scale
        scores = jnp.where(live, scores, -jnp.inf)
        row_max = lax.optimization_barrier(jnp.max(scores, axis=-1, keepdims=True))
        weights = jnp.exp(scores - row_max)
        probs = (weights / lax.optimization_barrier(jnp.sum(weights, axis=-1, keepdims=True))).astype(jnp.bfloat16)
        context = jnp.einsum('gqtc,cge->tgqe', probs.astype(jnp.float32), joined[:, :, 1])
        return context.astype(jnp.bfloat16).reshape(tree_size, H * HD)
    context = lax.map(attend, (query, tree_kv, kv_cache, lengths, ancestors))
    flat_context = context.reshape(requests * tree_size, H * HD)
    heads_width = H * HD // N_TP
    summed = jnp.zeros((requests * tree_size, full_width), jnp.float32)
    for group_index in range(N_TP):
        lower = group_index * heads_width
        partial_value = jnp.dot(flat_context[:, lower:lower + heads_width], w_out[lower:lower + heads_width], preferred_element_type=jnp.float32).astype(jnp.bfloat16)
        summed = summed + partial_value.astype(jnp.float32)
    out_rows = (values + summed.reshape(requests, tree_size, full_width)).astype(jnp.bfloat16)
    accepted_kv = jnp.transpose(jnp.take_along_axis(tree_kv, accepted[:, :, None], axis=1), (0, 2, 1))
    live_rows = positions[None, :] < lengths[:, None]
    kept = jnp.where(live_rows[:, None, :], kv_cache, jnp.zeros((), jnp.bfloat16))
    compacted = jax.vmap(place_columns)(kept, accepted_kv, lengths)
    new_cache = jnp.zeros_like(compacted).at[slot_of].set(compacted)
    return (out_rows, new_cache)
```

```python
import functools
import math

import jax
import jax.numpy as jnp
import numpy as np
from jax import lax
from jax.experimental import pallas as pl
from jax.experimental.pallas import tpu as pltpu
from jax.sharding import PartitionSpec as P

H = 32
KVH = 8
HD = 80
HALF = HD // 2
GROUP = H // KVH
MESH = pl.DeviceIdType.MESH
F32 = jnp.float32
BF16 = jnp.bfloat16
PAD = 16


def kernel(
    n, t, chunks, requests, tree,
    lengths, slots, accepted, hidden, gain, freq, parent, w_query, w_keyval, w_out, cache,
    out_rows, new_cache,
    wq, wkv, wo, kept, stage, landed, note_out, note_in, full, nrm, qs, kvs, marks, depth,
    ctx, part, terms,
    w_sem, cache_sem, ag_send, ag_recv, rs_send, rs_recv, move_send, move_recv,
    note_send, note_recv, out_sem,
):
    req, tp = lax.axis_index("req"), lax.axis_index("tp")
    rows, width = hidden.shape
    per = requests // chunks
    crows = per * tree
    cache_len = cache.shape[2]
    kv_local = wkv.shape[0] // (2 * HD)
    scale = 1.0 / math.sqrt(HD)

    def at_req(k):
        return lax.rem(req + k, n)

    def at_tp(k):
        return lax.rem(tp + k, t)

    def load_cache(r, carry):
        pltpu.make_async_copy(cache.at[r], kept.at[r], cache_sem.at[r]).start()
        return carry

    lax.fori_loop(0, requests, load_cache, 0)
    loads = [
        pltpu.make_async_copy(src, dst, w_sem.at[i])
        for i, (src, dst) in enumerate(((w_query, wq), (w_keyval, wkv), (w_out, wo)))
    ]
    for copy in loads:
        copy.start()

    barrier = pltpu.get_barrier_semaphore()
    for k in range(1, n):
        pl.semaphore_signal(barrier, inc=1, device_id=(at_req(k), tp), device_id_type=MESH)
    for k in range(1, t):
        pl.semaphore_signal(barrier, inc=1, device_id=(req, at_tp(k)), device_id_type=MESH)
    pl.semaphore_wait(barrier, n + t - 2)

    def gather_copy(c, k, slot):
        return pltpu.make_async_remote_copy(
            src_ref=hidden.at[pl.ds(c * crows, crows)],
            dst_ref=full.at[c, slot],
            send_sem=ag_send.at[c, k],
            recv_sem=ag_recv.at[c, slot],
            device_id=(req, at_tp(k)),
            device_id_type=MESH,
        )

    for c in range(chunks):
        for k in range(1, t):
            gather_copy(c, k, tp).start()
        full[c, tp] = hidden[c * crows : (c + 1) * crows]

    positions = lax.broadcasted_iota(jnp.int32, (1, cache_len), 1)

    def request_for(dest):
        def look(r, found):
            return jnp.where(slots[r] // requests == dest, r, found)

        return lax.fori_loop(0, requests, look, jnp.int32(0))

    def wait_cache(r, carry):
        pltpu.make_async_copy(cache.at[r], kept.at[r], cache_sem.at[r]).wait()
        return carry

    lax.fori_loop(0, requests, wait_cache, 0)

    def move_copy(k):
        return pltpu.make_async_remote_copy(
            src_ref=stage.at[k],
            dst_ref=landed.at[k],
            send_sem=move_send.at[k],
            recv_sem=move_recv.at[k],
            device_id=(at_req(k), tp),
            device_id_type=MESH,
        )

    def move(k, carry):
        r = request_for(at_req(k))
        stage[k] = jnp.where(positions < lengths[r], kept[r], jnp.zeros((), BF16))
        move_copy(k).start()
        return carry

    lax.fori_loop(1, n, move, 0)
    own = request_for(req)
    landed[0] = jnp.where(positions < lengths[own], kept[own], jnp.zeros((), BF16))

    seen = lax.broadcasted_iota(jnp.int32, (rows, rows), 1)
    line = lax.broadcasted_iota(jnp.int32, (rows, rows), 0)
    reach = jnp.logical_or(seen == parent[...], seen == line).astype(F32).astype(BF16)
    covered = 1
    while covered < tree:
        reach = jnp.minimum(jnp.dot(reach, reach, preferred_element_type=F32), 1.0).astype(BF16)
        covered *= 2
    fold = (
        lax.rem(lax.broadcasted_iota(jnp.int32, (rows, tree), 0), tree)
        == lax.broadcasted_iota(jnp.int32, (rows, tree), 1)
    ).astype(F32).astype(BF16)
    local = jnp.dot(reach, fold, preferred_element_type=F32)
    marks[...] = local.reshape(requests, tree, tree)
    depth[...] = (jnp.sum(local, axis=1, keepdims=True) - 1.0).reshape(requests, tree, 1)

    for copy in loads:
        copy.wait()

    def reduce_copy(c, k):
        return pltpu.make_async_remote_copy(
            src_ref=part.at[c, at_tp(k)],
            dst_ref=terms.at[c, tp],
            send_sem=rs_send.at[c, k],
            recv_sem=rs_recv.at[c, tp],
            device_id=(req, at_tp(k)),
            device_id_type=MESH,
        )

    def chunk(c, carry):
        for k in range(1, t):
            peer = at_tp(k)
            gather_copy(c, k, peer).wait_recv()
        spread = jnp.zeros((crows, 1), F32)
        for g in range(t):
            value = full[c, g].astype(F32)
            spread += jnp.sum(value * value, axis=1, keepdims=True)
        inverse = lax.rsqrt(spread / (t * width) + 1e-05)
        for g in range(t):
            value = full[c, g].astype(F32)
            nrm[:, g * width : (g + 1) * width] = (value * inverse * gain[g : g + 1, :]).astype(BF16)
        normed = nrm[...]
        query = jnp.dot(normed, wq[...], preferred_element_type=F32)
        keyval = lax.dot_general(
            normed, wkv[...], (((1,), (1,)), ((), ())), preferred_element_type=F32
        )
        place = jnp.concatenate(
            [depth[c * per + i] + lengths[c * per + i].astype(F32) for i in range(per)], axis=0
        )
        angles = place * freq[...]
        cosines, sines = jnp.cos(angles), jnp.sin(angles)

        def turn(value):
            first, second = value[:, :HALF], value[:, HALF:]
            return jnp.concatenate(
                [first * cosines - second * sines, second * cosines + first * sines], axis=1
            )

        for h in range(kv_local * GROUP):
            value = turn(query[:, h * HD : (h + 1) * HD])
            qs[h] = value.reshape(per, tree, HD)
        for i in range(2 * kv_local):
            value = keyval[:, i * HD : (i + 1) * HD]
            if i % 2 == 0:
                value = turn(value)
            value = value.astype(BF16).astype(F32).reshape(per, tree, HD)
            kvs[pl.ds(c * per, per), i] = value

        def attend(i, inner):
            r = c * per + i
            live = positions < lengths[r]
            mask = marks[r] > 0.5
            mask = jnp.concatenate([mask.astype(F32)] * GROUP, axis=0) > 0.5
            for g in range(kv_local):
                q = qs[g * GROUP : (g + 1) * GROUP, i].reshape(GROUP * tree, HD).astype(BF16)
                low = g * 2 * HD
                keys = kept[r, low : low + HD, :]
                values = kept[r, low + HD : low + 2 * HD, :]
                tree_keys = kvs[r, 2 * g].astype(BF16)
                tree_values = kvs[r, 2 * g + 1].astype(BF16)
                a = jnp.dot(q, keys, preferred_element_type=F32) * scale
                b = lax.dot_general(
                    q, tree_keys, (((1,), (1,)), ((), ())), preferred_element_type=F32
                ) * scale
                a = jnp.where(live, a, -1e30)
                b = jnp.where(mask, b, -1e30)
                top = jnp.maximum(
                    jnp.max(a, axis=1, keepdims=True), jnp.max(b, axis=1, keepdims=True)
                )
                a, b = jnp.exp(a - top), jnp.exp(b - top)
                total = jnp.sum(a, axis=1, keepdims=True) + jnp.sum(b, axis=1, keepdims=True)
                inverse_total = 1.0 / total
                a = (a * inverse_total).astype(BF16)
                b = (b * inverse_total).astype(BF16)
                value = lax.dot_general(
                    a, values, (((1,), (1,)), ((), ())), preferred_element_type=F32
                ) + jnp.dot(b, tree_values, preferred_element_type=F32)
                for j in range(GROUP):
                    h = g * GROUP + j
                    ctx[i, :, h * HD : (h + 1) * HD] = value[j * tree : (j + 1) * tree]
            return inner

        lax.fori_loop(0, per, attend, 0)
        rounded = ctx[...].reshape(crows, kv_local * GROUP * HD).astype(BF16)
        for g in range(t):
            part[c, g] = jnp.dot(
                rounded, wo[:, g * width : (g + 1) * width], preferred_element_type=F32
            ).astype(BF16)
        for k in range(1, t):
            reduce_copy(c, k).start()
        terms[c, tp] = part[c, tp]
        return carry

    lax.fori_loop(0, chunks, chunk, 0)

    level = lax.broadcasted_iota(jnp.int32, (PAD, tree), 0)
    token = lax.broadcasted_iota(jnp.int32, (PAD, tree), 1)
    level_c = lax.broadcasted_iota(jnp.int32, (PAD, cache_len), 0)
    place_c = lax.broadcasted_iota(jnp.int32, (PAD, cache_len), 1)
    n_accept = accepted.shape[1]

    def write_note(k, target):
        r = request_for(at_req(k))
        pick = jnp.zeros((PAD, tree), F32)
        for m in range(n_accept):
            hit = jnp.logical_and(level == m, token == accepted[r, m])
            pick = jnp.where(hit, 1.0, pick)
        pick = pick.astype(BF16)
        spot = jnp.logical_and(place_c == level_c + lengths[r], level_c < n_accept)
        target[k, 0:PAD, :] = spot.astype(F32).astype(BF16)
        chosen = [
            jnp.dot(pick, kvs[r, i].astype(BF16), preferred_element_type=F32)
            for i in range(2 * kv_local)
        ]
        chosen = jnp.concatenate(chosen, axis=1).astype(BF16)
        target[k, PAD : 2 * PAD, 0 : 2 * kv_local * HD] = chosen

    def note_copy(k):
        return pltpu.make_async_remote_copy(
            src_ref=note_out.at[k],
            dst_ref=note_in.at[k],
            send_sem=note_send.at[k],
            recv_sem=note_recv.at[k],
            device_id=(at_req(k), tp),
            device_id_type=MESH,
        )

    def send_note(k, carry):
        write_note(k, note_out)
        note_copy(k).start()
        return carry

    note_out[...] = jnp.zeros_like(note_out)
    lax.fori_loop(1, n, send_note, 0)
    note_in[0] = jnp.zeros_like(note_in[0])
    write_note(0, note_in)

    def out_copy(k):
        return pltpu.make_async_copy(
            landed.at[k], new_cache.at[lax.rem(req + n - k, n)], out_sem.at[k]
        )

    def finish(k):
        spot = note_in[k, 0:PAD, :]
        chosen = note_in[k, PAD : 2 * PAD, 0 : 2 * kv_local * HD]
        added = lax.dot_general(chosen, spot, (((0,), (0,)), ((), ())), preferred_element_type=F32)
        landed[k] = landed[k] + added.astype(BF16)
        out_copy(k).start()

    finish(0)

    def receive(k, carry):
        move_copy(k).wait_recv()
        note_copy(k).wait_recv()
        finish(k)
        return carry

    lax.fori_loop(1, n, receive, 0)

    def close(c, carry):
        for k in range(1, t):
            peer = at_tp(k)
            pltpu.make_async_remote_copy(
                src_ref=part.at[c, peer],
                dst_ref=terms.at[c, peer],
                send_sem=rs_send.at[c, k],
                recv_sem=rs_recv.at[c, peer],
                device_id=(req, peer),
                device_id_type=MESH,
            ).wait_recv()
        summed = terms[c, 0].astype(F32)
        for g in range(1, t):
            summed += terms[c, g].astype(F32)
        where = pl.ds(pl.multiple_of(c * crows, 16), crows)
        out_rows[where, :] = (hidden[where, :].astype(F32) + summed).astype(BF16)
        return carry

    lax.fori_loop(0, chunks, close, 0)

    for c in range(chunks):
        for k in range(1, t):
            gather_copy(c, k, tp).wait_send()
            reduce_copy(c, k).wait_send()

    def drain(k, carry):
        move_copy(k).wait_send()
        note_copy(k).wait_send()
        out_copy(k).wait()
        return carry

    lax.fori_loop(1, n, drain, 0)
    out_copy(0).wait()


def per_device(
    n, t,
    hidden, norm_gain, w_query, w_keyval, w_out, kv_cache, lengths, parents, accepted, slot_of
):
    requests, tree, width = hidden.shape
    rows = requests * tree
    features = w_query.shape[0]
    q_width = w_query.shape[1]
    kv_rows = w_keyval.shape[0]
    cache_len = kv_cache.shape[2]
    chunks = 2
    per = requests // chunks
    crows = per * tree
    heads = q_width // HD
    freq = jnp.asarray(
        (10000.0 ** (-2.0 * np.arange(HALF, dtype=np.float64) / HD)).astype(np.float32)
    ).reshape(1, HALF)
    parent = (parents + tree * jnp.arange(requests, dtype=jnp.int32)[:, None]).reshape(rows, 1)
    smem = pl.BlockSpec(memory_space=pltpu.SMEM)
    vmem = pl.BlockSpec(memory_space=pltpu.VMEM)
    hbm = pl.BlockSpec(memory_space=pl.ANY)
    dma = pltpu.SemaphoreType.DMA
    out_rows, new_cache = pl.pallas_call(
        functools.partial(kernel, n, t, chunks, requests, tree),
        out_shape=(
            jax.ShapeDtypeStruct((rows, width), BF16),
            jax.ShapeDtypeStruct(kv_cache.shape, BF16),
        ),
        in_specs=[smem] * 3 + [vmem] * 4 + [hbm] * 4,
        out_specs=(vmem, hbm),
        scratch_shapes=[
            pltpu.VMEM(w_query.shape, BF16),
            pltpu.VMEM(w_keyval.shape, BF16),
            pltpu.VMEM(w_out.shape, BF16),
            pltpu.VMEM(kv_cache.shape, BF16),
            pltpu.VMEM((n,) + kv_cache.shape[1:], BF16),
            pltpu.VMEM((n,) + kv_cache.shape[1:], BF16),
            pltpu.VMEM((n, 2 * PAD, cache_len), BF16),
            pltpu.VMEM((n, 2 * PAD, cache_len), BF16),
            pltpu.VMEM((chunks, t, crows, width), BF16),
            pltpu.VMEM((crows, features), BF16),
            pltpu.VMEM((heads, per, tree, HD), F32),
            pltpu.VMEM((requests, kv_rows // HD, tree, HD), F32),
            pltpu.VMEM((requests, tree, tree), F32),
            pltpu.VMEM((requests, tree, 1), F32),
            pltpu.VMEM((per, tree, q_width), F32),
            pltpu.VMEM((chunks, t, crows, width), BF16),
            pltpu.VMEM((chunks, t, crows, width), BF16),
            dma((3,)),
            dma((requests,)),
            dma((chunks, t)),
            dma((chunks, t)),
            dma((chunks, t)),
            dma((chunks, t)),
            dma((n,)),
            dma((n,)),
            dma((n,)),
            dma((n,)),
            dma((n,)),
        ],
        compiler_params=pltpu.CompilerParams(
            collective_id=0, has_side_effects=True, vmem_limit_bytes=56 * 1024 * 1024
        ),
    )(
        lengths, slot_of, accepted, hidden.reshape(rows, width), norm_gain.reshape(t, width),
        freq, parent, w_query, w_keyval, w_out, kv_cache,
    )
    return (out_rows.reshape(requests, tree, width), new_cache)


def solution(mesh):
    in_specs = (
        P("req", None, "tp"),
        P(),
        P(None, "tp"),
        P("tp", None),
        P("tp", None),
        P("req", "tp", None),
        P("req"),
        P("req", None),
        P("req", None),
        P("req"),
    )
    out_specs = (P("req", None, "tp"), P("req", "tp", None))
    return jax.shard_map(
        functools.partial(per_device, mesh.shape["req"], mesh.shape["tp"]),
        mesh=mesh, in_specs=in_specs, out_specs=out_specs, check_vma=False,
    )
```

```python
import functools
import math

import jax
import jax.numpy as jnp
import numpy as np
from jax import lax
from jax.experimental import pallas as pl
from jax.experimental.pallas import tpu as pltpu
from jax.sharding import PartitionSpec as P

H = 32
KVH = 8
HD = 80
HALF = HD // 2
GROUP = H // KVH
MESH = pl.DeviceIdType.MESH
F32 = jnp.float32
BF16 = jnp.bfloat16
PAD = 16


def kernel(
    n, t, chunks, requests, tree,
    lengths, slots, accepted, hidden, gain, freq, parent, w_query, w_keyval, w_out, cache,
    out_rows, new_cache,
    wq, wkv, wo, kept, stage, landed, note_out, note_in, full, nrm, qs, kvs, marks, depth,
    ctx, part, outgoing, incoming, total,
    w_sem, cache_sem, ag_send, ag_recv, rs_send, rs_recv, move_send, move_recv,
    note_send, note_recv, out_sem,
):
    req, tp = lax.axis_index("req"), lax.axis_index("tp")
    rows, width = hidden.shape
    per = requests // chunks
    crows = per * tree
    cache_len = cache.shape[2]
    kv_local = wkv.shape[0] // (2 * HD)
    scale = 1.0 / math.sqrt(HD)

    def at_req(k):
        return lax.rem(req + k, n)

    def at_tp(k):
        return lax.rem(tp + k, t)

    def load_cache(r, carry):
        pltpu.make_async_copy(cache.at[r], kept.at[r], cache_sem.at[r]).start()
        return carry

    lax.fori_loop(0, requests, load_cache, 0)
    loads = [
        pltpu.make_async_copy(src, dst, w_sem.at[i])
        for i, (src, dst) in enumerate(((w_query, wq), (w_keyval, wkv), (w_out, wo)))
    ]
    for copy in loads:
        copy.start()

    barrier = pltpu.get_barrier_semaphore()
    for k in range(1, n):
        pl.semaphore_signal(barrier, inc=1, device_id=(at_req(k), tp), device_id_type=MESH)

    @pl.when(tp > 0)
    def _():
        pl.semaphore_signal(barrier, inc=1, device_id=(req, tp - 1), device_id_type=MESH)

    @pl.when(tp < t - 1)
    def _():
        pl.semaphore_signal(barrier, inc=1, device_id=(req, tp + 1), device_id_type=MESH)

    neighbours = (tp > 0).astype(jnp.int32) + (tp < t - 1).astype(jnp.int32)
    pl.semaphore_wait(barrier, n - 1 + neighbours)

    def ends(up):
        behind = tp if up else t - 1 - tp
        return behind, behind < t - 1, 1 if up else -1

    def gather_copy(c, s, up, arriving=False):
        behind, more, ahead = ends(up)
        slot = tp - ahead * (s + 1) if arriving else tp - ahead * s
        peer = tp - ahead if arriving else tp + ahead
        way = 0 if up else 1
        return pltpu.make_async_remote_copy(
            src_ref=full.at[c, slot],
            dst_ref=full.at[c, slot],
            send_sem=ag_send.at[way, c, s],
            recv_sem=ag_recv.at[way, c, s],
            device_id=(req, peer),
            device_id_type=MESH,
        )

    def gather_start(c):
        full[c, tp] = hidden[c * crows : (c + 1) * crows]
        for up in (True, False):
            behind, more, ahead = ends(up)

            @pl.when(more)
            def _():
                gather_copy(c, 0, up).start()

    def gather_step(c, s):
        for up in (True, False):
            behind, more, ahead = ends(up)

            @pl.when(behind >= s)
            def _():
                gather_copy(c, s - 1, up, arriving=True).wait_recv()

            if s < t - 1:

                @pl.when(jnp.logical_and(behind >= s, more))
                def _():
                    gather_copy(c, s, up).start()

    gather_start(0)
    gains = gain[...].reshape(1, t * width)

    positions = lax.broadcasted_iota(jnp.int32, (1, cache_len), 1)

    def request_for(dest):
        def look(r, found):
            return jnp.where(slots[r] // requests == dest, r, found)

        return lax.fori_loop(0, requests, look, jnp.int32(0))

    def wait_cache(r, carry):
        pltpu.make_async_copy(cache.at[r], kept.at[r], cache_sem.at[r]).wait()
        return carry

    lax.fori_loop(0, requests, wait_cache, 0)

    def move_copy(k):
        return pltpu.make_async_remote_copy(
            src_ref=stage.at[k],
            dst_ref=landed.at[k],
            send_sem=move_send.at[k],
            recv_sem=move_recv.at[k],
            device_id=(at_req(k), tp),
            device_id_type=MESH,
        )

    def move(k, carry):
        r = request_for(at_req(k))
        stage[k] = jnp.where(positions < lengths[r], kept[r], jnp.zeros((), BF16))
        move_copy(k).start()
        return carry

    lax.fori_loop(1, n, move, 0)
    own = request_for(req)
    landed[0] = jnp.where(positions < lengths[own], kept[own], jnp.zeros((), BF16))

    if t > 1:
        gather_step(0, 1)
    if chunks > 1:
        gather_start(1)

    seen = lax.broadcasted_iota(jnp.int32, (rows, rows), 0)
    line = lax.broadcasted_iota(jnp.int32, (rows, rows), 1)
    parent_row = jnp.concatenate(
        [parent[r : r + 1, :] + r * tree for r in range(requests)], axis=1
    )
    reach = jnp.logical_or(seen == parent_row, seen == line).astype(F32).astype(BF16)
    covered = 1
    while covered < tree:
        reach = jnp.minimum(jnp.dot(reach, reach, preferred_element_type=F32), 1.0).astype(BF16)
        covered *= 2
    fold = (
        lax.rem(lax.broadcasted_iota(jnp.int32, (rows, tree), 0), tree)
        == lax.broadcasted_iota(jnp.int32, (rows, tree), 1)
    ).astype(F32).astype(BF16)
    local = lax.dot_general(reach, fold, (((0,), (0,)), ((), ())), preferred_element_type=F32)
    marks[...] = local.reshape(requests, tree, tree)
    depth[...] = (jnp.sum(local, axis=1, keepdims=True) - 1.0).reshape(requests, tree, 1)

    for s in range(2, t):
        gather_step(0, s)

    for copy in loads:
        copy.wait()

    def reduce_copy(c, g, up, arriving=False):
        behind, more, ahead = ends(up)
        way = 0 if up else 1
        return pltpu.make_async_remote_copy(
            src_ref=outgoing.at[c, g],
            dst_ref=incoming.at[way, c, g],
            send_sem=rs_send.at[c, g],
            recv_sem=rs_recv.at[way, c, g],
            device_id=(req, tp - ahead if arriving else tp + ahead),
            device_id_type=MESH,
        )

    def reduce_step(c, q):
        for up in (True, False):
            behind, more, ahead = ends(up)
            g = t - 1 - q if up else q
            way = 0 if up else 1
            mine = g > tp if up else g < tp

            @pl.when(jnp.logical_and(mine, behind == 0))
            def _():
                outgoing[c, g] = part[c, g]
                reduce_copy(c, g, up).start()

            @pl.when(jnp.logical_and(mine, behind > 0))
            def _():
                reduce_copy(c, g, up, arriving=True).wait_recv()
                outgoing[c, g] = (
                    part[c, g].astype(F32) + incoming[way, c, g].astype(F32)
                ).astype(BF16)
                reduce_copy(c, g, up).start()

    def spread_steps(action, c, first, last, third):
        steps = list(range(first, last))
        for s in steps[len(steps) * third // 3 : len(steps) * (third + 1) // 3]:
            action(c, s)

    def pump(c, third):
        if c + 1 < chunks:
            spread_steps(gather_step, c + 1, 1, t, third)
        if c > 0:
            spread_steps(reduce_step, c - 1, 0, t - 1, third)

    def chunk(c):
        if 0 < c < chunks - 1:
            gather_start(c + 1)
        spread = jnp.zeros((crows, 1), F32)
        for g in range(t):
            value = full[c, g].astype(F32)
            spread += jnp.sum(value * value, axis=1, keepdims=True)
        inverse = lax.rsqrt(spread / (t * width) + 1e-05)
        for g in range(t):
            value = full[c, g].astype(F32)
            nrm[:, g * width : (g + 1) * width] = (value * inverse * gains[:, g * width : (g + 1) * width]).astype(BF16)
        normed = nrm[...]
        query = jnp.dot(normed, wq[...], preferred_element_type=F32)
        keyval = lax.dot_general(
            normed, wkv[...], (((1,), (1,)), ((), ())), preferred_element_type=F32
        )
        place = jnp.concatenate(
            [depth[c * per + i] + lengths[c * per + i].astype(F32) for i in range(per)], axis=0
        )
        angles = place * freq[...]
        cosines, sines = jnp.cos(angles), jnp.sin(angles)

        pump(c, 0)

        def turn(value):
            first, second = value[:, :HALF], value[:, HALF:]
            return jnp.concatenate(
                [first * cosines - second * sines, second * cosines + first * sines], axis=1
            )

        for h in range(kv_local * GROUP):
            value = turn(query[:, h * HD : (h + 1) * HD])
            qs[h] = value.reshape(per, tree, HD)
        for i in range(2 * kv_local):
            value = keyval[:, i * HD : (i + 1) * HD]
            if i % 2 == 0:
                value = turn(value)
            value = value.astype(BF16).astype(F32).reshape(per, tree, HD)
            kvs[pl.ds(c * per, per), i] = value

        def attend(i, inner):
            r = c * per + i
            live = positions < lengths[r]
            mask = marks[r] > 0.5
            mask = jnp.concatenate([mask.astype(F32)] * GROUP, axis=0) > 0.5
            for g in range(kv_local):
                q = qs[g * GROUP : (g + 1) * GROUP, i].reshape(GROUP * tree, HD).astype(BF16)
                low = g * 2 * HD
                keys = kept[r, low : low + HD, :]
                values = kept[r, low + HD : low + 2 * HD, :]
                tree_keys = kvs[r, 2 * g].astype(BF16)
                tree_values = kvs[r, 2 * g + 1].astype(BF16)
                a = jnp.dot(q, keys, preferred_element_type=F32) * scale
                b = lax.dot_general(
                    q, tree_keys, (((1,), (1,)), ((), ())), preferred_element_type=F32
                ) * scale
                a = jnp.where(live, a, -1e30)
                b = jnp.where(mask, b, -1e30)
                top = jnp.maximum(
                    jnp.max(a, axis=1, keepdims=True), jnp.max(b, axis=1, keepdims=True)
                )
                a, b = jnp.exp(a - top), jnp.exp(b - top)
                total = jnp.sum(a, axis=1, keepdims=True) + jnp.sum(b, axis=1, keepdims=True)
                inverse_total = 1.0 / total
                a = (a * inverse_total).astype(BF16)
                b = (b * inverse_total).astype(BF16)
                value = lax.dot_general(
                    a, values, (((1,), (1,)), ((), ())), preferred_element_type=F32
                ) + jnp.dot(b, tree_values, preferred_element_type=F32)
                for j in range(GROUP):
                    h = g * GROUP + j
                    ctx[i, :, h * HD : (h + 1) * HD] = value[j * tree : (j + 1) * tree]
            return inner

        lax.fori_loop(0, per // 2, attend, 0)
        pump(c, 1)
        lax.fori_loop(per // 2, per, attend, 0)
        pump(c, 2)
        rounded = ctx[...].reshape(crows, kv_local * GROUP * HD).astype(BF16)
        for g in range(t):
            part[c, g] = jnp.dot(
                rounded, wo[:, g * width : (g + 1) * width], preferred_element_type=F32
            ).astype(BF16)

    for c in range(chunks):
        chunk(c)
    reduce_step(chunks - 1, 0)

    level_c = lax.broadcasted_iota(jnp.int32, (PAD, cache_len), 0)
    place_c = lax.broadcasted_iota(jnp.int32, (PAD, cache_len), 1)
    n_accept = accepted.shape[0]
    token = lax.broadcasted_iota(jnp.int32, (n_accept, tree), 1)
    asked = lax.broadcasted_iota(jnp.int32, accepted.shape, 1)

    def write_note(k, target):
        r = request_for(at_req(k))
        path = jnp.sum(jnp.where(asked == r, accepted[...], 0), axis=1, keepdims=True)
        pick = (token == path).astype(F32)
        pick = jnp.concatenate([pick, jnp.zeros((PAD - n_accept, tree), F32)], axis=0).astype(BF16)
        spot = jnp.logical_and(place_c == level_c + lengths[r], level_c < n_accept)
        target[k, 0:PAD, :] = spot.astype(F32).astype(BF16)
        chosen = [
            jnp.dot(pick, kvs[r, i].astype(BF16), preferred_element_type=F32)
            for i in range(2 * kv_local)
        ]
        chosen = jnp.concatenate(chosen, axis=1).astype(BF16)
        target[k, PAD : 2 * PAD, 0 : 2 * kv_local * HD] = chosen

    def note_copy(k):
        return pltpu.make_async_remote_copy(
            src_ref=note_out.at[k],
            dst_ref=note_in.at[k],
            send_sem=note_send.at[k],
            recv_sem=note_recv.at[k],
            device_id=(at_req(k), tp),
            device_id_type=MESH,
        )

    def send_note(k, carry):
        write_note(k, note_out)
        note_copy(k).start()
        return carry

    note_out[...] = jnp.zeros_like(note_out)
    lax.fori_loop(1, n, send_note, 0)
    note_in[0] = jnp.zeros_like(note_in[0])
    write_note(0, note_in)

    def out_copy(k):
        return pltpu.make_async_copy(
            landed.at[k], new_cache.at[lax.rem(req + n - k, n)], out_sem.at[k]
        )

    def finish(k):
        spot = note_in[k, 0:PAD, :]
        chosen = note_in[k, PAD : 2 * PAD, 0 : 2 * kv_local * HD]
        added = lax.dot_general(chosen, spot, (((0,), (0,)), ((), ())), preferred_element_type=F32)
        landed[k] = landed[k] + added.astype(BF16)
        out_copy(k).start()

    finish(0)
    for q in range(1, t - 1):
        reduce_step(chunks - 1, q)

    def receive(k, carry):
        move_copy(k).wait_recv()
        note_copy(k).wait_recv()
        finish(k)
        return carry

    lax.fori_loop(1, n, receive, 0)

    def close(c, carry):
        where = pl.ds(pl.multiple_of(c * crows, 16), crows)
        total[...] = part[c, tp].astype(F32) + hidden[where, :].astype(F32)
        for up in (True, False):
            behind, more, ahead = ends(up)

            @pl.when(behind > 0)
            def _():
                reduce_copy(c, tp, up, arriving=True).wait_recv()
                total[...] += incoming[0 if up else 1, c, tp].astype(F32)

        out_rows[where, :] = total[...].astype(BF16)
        return carry

    lax.fori_loop(0, chunks, close, 0)

    for c in range(chunks):
        for up in (True, False):
            behind, more, ahead = ends(up)
            for s in range(t - 1):

                @pl.when(jnp.logical_and(behind >= s, more))
                def _():
                    gather_copy(c, s, up).wait_send()

        for g in range(t):

            @pl.when(g > tp)
            def _():
                reduce_copy(c, g, True).wait_send()

            @pl.when(g < tp)
            def _():
                reduce_copy(c, g, False).wait_send()

    def drain(k, carry):
        move_copy(k).wait_send()
        note_copy(k).wait_send()
        out_copy(k).wait()
        return carry

    lax.fori_loop(1, n, drain, 0)
    out_copy(0).wait()


def hand_over(rows, cache, out_rows, new_cache, sem):
    count = cache.shape[0]
    copies = [pltpu.make_async_copy(cache.at[i], new_cache.at[i], sem.at[i]) for i in range(count)]
    copies.append(pltpu.make_async_copy(rows, out_rows, sem.at[count]))
    for copy in copies:
        copy.start()
    for copy in copies:
        copy.wait()


def per_device(
    n, t,
    hidden, norm_gain, w_query, w_keyval, w_out, kv_cache, lengths, parents, accepted, slot_of
):
    requests, tree, width = hidden.shape
    rows = requests * tree
    features = w_query.shape[0]
    q_width = w_query.shape[1]
    kv_rows = w_keyval.shape[0]
    cache_len = kv_cache.shape[2]
    chunks = 2
    per = requests // chunks
    crows = per * tree
    heads = q_width // HD
    freq = jnp.asarray(
        (10000.0 ** (-2.0 * np.arange(HALF, dtype=np.float64) / HD)).astype(np.float32)
    ).reshape(1, HALF)
    smem = pl.BlockSpec(memory_space=pltpu.SMEM)
    vmem = pl.BlockSpec(memory_space=pltpu.VMEM)
    hbm = pl.BlockSpec(memory_space=pl.ANY)
    dma = pltpu.SemaphoreType.DMA
    out_rows, new_cache = pl.pallas_call(
        functools.partial(kernel, n, t, chunks, requests, tree),
        out_shape=(
            jax.ShapeDtypeStruct((rows, width), BF16),
            jax.ShapeDtypeStruct(kv_cache.shape, BF16),
        ),
        in_specs=[smem] * 2 + [vmem] * 5 + [hbm] * 4,
        out_specs=(vmem, hbm),
        scratch_shapes=[
            pltpu.VMEM(w_query.shape, BF16),
            pltpu.VMEM(w_keyval.shape, BF16),
            pltpu.VMEM(w_out.shape, BF16),
            pltpu.VMEM(kv_cache.shape, BF16),
            pltpu.VMEM((n,) + kv_cache.shape[1:], BF16),
            pltpu.VMEM((n,) + kv_cache.shape[1:], BF16),
            pltpu.VMEM((n, 2 * PAD, cache_len), BF16),
            pltpu.VMEM((n, 2 * PAD, cache_len), BF16),
            pltpu.VMEM((chunks, t, crows, width), BF16),
            pltpu.VMEM((crows, features), BF16),
            pltpu.VMEM((heads, per, tree, HD), F32),
            pltpu.VMEM((requests, kv_rows // HD, tree, HD), F32),
            pltpu.VMEM((requests, tree, tree), F32),
            pltpu.VMEM((requests, tree, 1), F32),
            pltpu.VMEM((per, tree, q_width), F32),
            pltpu.VMEM((chunks, t, crows, width), BF16),
            pltpu.VMEM((chunks, t, crows, width), BF16),
            pltpu.VMEM((2, chunks, t, crows, width), BF16),
            pltpu.VMEM((crows, width), F32),
            dma((3,)),
            dma((requests,)),
            dma((2, chunks, t)),
            dma((2, chunks, t)),
            dma((chunks, t)),
            dma((2, chunks, t)),
            dma((n,)),
            dma((n,)),
            dma((n,)),
            dma((n,)),
            dma((n,)),
        ],
        compiler_params=pltpu.CompilerParams(
            collective_id=0, has_side_effects=True, vmem_limit_bytes=56 * 1024 * 1024
        ),
    )(
        lengths, slot_of, accepted.T, hidden.reshape(rows, width), norm_gain,
        freq, parents, w_query, w_keyval, w_out, kv_cache,
    )
    rows_shape, cache_shape = out_rows.shape, new_cache.shape
    out_rows, new_cache = pl.pallas_call(
        hand_over,
        out_shape=(
            jax.ShapeDtypeStruct(rows_shape, BF16),
            jax.ShapeDtypeStruct(cache_shape, BF16),
        ),
        in_specs=[hbm, hbm],
        out_specs=(hbm, hbm),
        scratch_shapes=[dma((cache_shape[0] + 1,))],
        compiler_params=pltpu.CompilerParams(vmem_limit_bytes=60 * 1024 * 1024),
    )(out_rows, new_cache)
    return (out_rows.reshape(requests, tree, width), new_cache)


def solution(mesh):
    in_specs = (
        P("req", None, "tp"),
        P(),
        P(None, "tp"),
        P("tp", None),
        P("tp", None),
        P("req", "tp", None),
        P("req"),
        P("req", None),
        P("req", None),
        P("req"),
    )
    out_specs = (P("req", None, "tp"), P("req", "tp", None))
    return jax.shard_map(
        functools.partial(per_device, mesh.shape["req"], mesh.shape["tp"]),
        mesh=mesh, in_specs=in_specs, out_specs=out_specs, check_vma=False,
    )
```

```python
import functools
import math

import jax
import jax.numpy as jnp
import numpy as np
from jax import lax
from jax.experimental import pallas as pl
from jax.experimental.pallas import tpu as pltpu
from jax.sharding import PartitionSpec as P

H = 32
KVH = 8
HD = 80
HALF = HD // 2
GROUP = H // KVH
MESH = pl.DeviceIdType.MESH
F32 = jnp.float32
BF16 = jnp.bfloat16
PAD = 16


def kernel(
    n, t, chunks, requests, tree,
    lengths, slots, accepted, hidden, gain, freq, parent, w_query, w_keyval, w_out, cache,
    out_rows, new_cache,
    wq, wkv, wo, kept, stage, landed, note_out, note_in, full, nrm, qs, kvs, marks, depth,
    ctx, part, outgoing, incoming, turns,
    w_sem, cache_sem, ag_send, ag_recv, rs_send, rs_recv, move_send, move_recv,
    note_send, note_recv, out_sem,
):
    req, tp = lax.axis_index("req"), lax.axis_index("tp")
    rows, width = hidden.shape
    per = requests // chunks
    crows = per * tree
    cache_len = cache.shape[2]
    kv_local = wkv.shape[0] // (2 * HD)
    scale = 1.0 / math.sqrt(HD)

    def at_req(k):
        return lax.rem(req + k, n)

    def at_tp(k):
        return lax.rem(tp + k, t)

    def load_cache(r, carry):
        pltpu.make_async_copy(cache.at[r], kept.at[r], cache_sem.at[r]).start()
        return carry

    lax.fori_loop(0, requests, load_cache, 0)
    loads = [
        pltpu.make_async_copy(src, dst, w_sem.at[i])
        for i, (src, dst) in enumerate(((w_query, wq), (w_keyval, wkv), (w_out, wo)))
    ]
    for copy in loads:
        copy.start()

    barrier = pltpu.get_barrier_semaphore()
    for k in range(1, n):
        pl.semaphore_signal(barrier, inc=1, device_id=(at_req(k), tp), device_id_type=MESH)

    strides = [1 << j for j in range(t.bit_length() - 1)]

    def flip(m):
        place = tp
        for b in strides:
            if m & b:
                place = place + b * (1 - 2 * lax.rem(tp // b, 2))
        return place

    for b in strides:
        pl.semaphore_signal(barrier, inc=1, device_id=(req, flip(b)), device_id_type=MESH)
    pl.semaphore_wait(barrier, n - 1 + len(strides))

    def low(m):
        return m & -m

    def gather_copy(c, m, b):
        slot = flip(m)
        return pltpu.make_async_remote_copy(
            src_ref=full.at[c, slot],
            dst_ref=full.at[c, slot],
            send_sem=ag_send.at[c, m | b],
            recv_sem=ag_recv.at[c, m | b],
            device_id=(req, flip(b)),
            device_id_type=MESH,
        )

    def gather_start(c):
        full[c, tp] = hidden[c * crows : (c + 1) * crows]
        for b in reversed(strides):
            gather_copy(c, 0, b).start()

    def gather_wait(c, m):
        slot = flip(m)
        pltpu.make_async_remote_copy(
            src_ref=full.at[c, slot],
            dst_ref=full.at[c, slot],
            send_sem=ag_send.at[c, m],
            recv_sem=ag_recv.at[c, m],
            device_id=(req, flip(low(m))),
            device_id_type=MESH,
        ).wait_recv()

    passed_on = sorted((m for m in range(2, t) if low(m) > 1), key=low, reverse=True)

    def gather_pass(c):
        for m in passed_on:
            gather_wait(c, m)
            for b in reversed(strides):
                if b < low(m):
                    gather_copy(c, m, b).start()

    def gather_end(c):
        for m in range(1, t, 2):
            gather_wait(c, m)

    for c in range(chunks):
        gather_start(c)
    gains = gain[...].reshape(1, t * width)

    positions = lax.broadcasted_iota(jnp.int32, (1, cache_len), 1)

    def request_for(dest):
        def look(r, found):
            return jnp.where(slots[r] // requests == dest, r, found)

        return lax.fori_loop(0, requests, look, jnp.int32(0))

    def wait_cache(r, carry):
        pltpu.make_async_copy(cache.at[r], kept.at[r], cache_sem.at[r]).wait()
        return carry

    lax.fori_loop(0, requests, wait_cache, 0)

    def move_copy(k):
        return pltpu.make_async_remote_copy(
            src_ref=stage.at[k],
            dst_ref=landed.at[k],
            send_sem=move_send.at[k],
            recv_sem=move_recv.at[k],
            device_id=(at_req(k), tp),
            device_id_type=MESH,
        )

    def move(k, carry):
        r = request_for(at_req(k))
        stage[k] = jnp.where(positions < lengths[r], kept[r], jnp.zeros((), BF16))
        move_copy(k).start()
        return carry

    lax.fori_loop(1, n, move, 0)
    own = request_for(req)
    landed[0] = jnp.where(positions < lengths[own], kept[own], jnp.zeros((), BF16))

    gather_pass(0)

    seen = lax.broadcasted_iota(jnp.int32, (rows, rows), 0)
    line = lax.broadcasted_iota(jnp.int32, (rows, rows), 1)
    parent_row = jnp.concatenate(
        [parent[r : r + 1, :] + r * tree for r in range(requests)], axis=1
    )
    reach = jnp.logical_or(seen == parent_row, seen == line).astype(F32).astype(BF16)
    covered = 1
    while covered < tree:
        reach = jnp.minimum(jnp.dot(reach, reach, preferred_element_type=F32), 1.0).astype(BF16)
        covered *= 2
    fold = (
        lax.rem(lax.broadcasted_iota(jnp.int32, (rows, tree), 0), tree)
        == lax.broadcasted_iota(jnp.int32, (rows, tree), 1)
    ).astype(F32).astype(BF16)
    local = lax.dot_general(reach, fold, (((0,), (0,)), ((), ())), preferred_element_type=F32)
    marks[...] = local.reshape(requests, tree, tree)
    depth[...] = (jnp.sum(local, axis=1, keepdims=True) - 1.0).reshape(requests, tree, 1)

    for r in range(requests):
        angles = (depth[r] + lengths[r].astype(F32)) * freq[...]
        turns[0, r] = jnp.cos(angles)
        turns[1, r] = jnp.sin(angles)

    for copy in loads:
        copy.wait()

    def reduce_copy(c, m):
        return pltpu.make_async_remote_copy(
            src_ref=outgoing.at[c, m],
            dst_ref=incoming.at[c, m],
            send_sem=rs_send.at[c, m],
            recv_sem=rs_recv.at[c, m],
            device_id=(req, flip(low(m))),
            device_id_type=MESH,
        )

    def reduce_sum(c, m):
        value = part[c, flip(m)].astype(F32)
        for b in strides:
            if m == 0 or b < low(m):
                reduce_copy(c, m | b).wait_recv()
                value += incoming[c, m | b].astype(F32)
        return value

    def reduce_start(c):
        for m in range(t - 1, 0, -2):
            outgoing[c, m] = part[c, flip(m)]
            reduce_copy(c, m).start()

    def reduce_pass(c):
        for m in sorted(passed_on, key=low):
            outgoing[c, m] = reduce_sum(c, m).astype(BF16)
            reduce_copy(c, m).start()

    def chunk(c):
        if c > 0:
            gather_pass(c)
        gather_end(c)
        spread = jnp.zeros((crows, 1), F32)
        for g in range(t):
            value = full[c, g].astype(F32)
            spread += jnp.sum(value * value, axis=1, keepdims=True)
        inverse = lax.rsqrt(spread / (t * width) + 1e-05)
        for g in range(t):
            value = full[c, g].astype(F32)
            nrm[:, g * width : (g + 1) * width] = (value * inverse * gains[:, g * width : (g + 1) * width]).astype(BF16)
        normed = nrm[...]
        query = jnp.dot(normed, wq[...], preferred_element_type=F32)
        keyval = lax.dot_general(
            normed, wkv[...], (((1,), (1,)), ((), ())), preferred_element_type=F32
        )
        if c > 0:
            reduce_pass(c - 1)
        cosines = turns[0, c * per : (c + 1) * per].reshape(crows, HALF)
        sines = turns[1, c * per : (c + 1) * per].reshape(crows, HALF)

        def turn(value):
            first, second = value[:, :HALF], value[:, HALF:]
            return jnp.concatenate(
                [first * cosines - second * sines, second * cosines + first * sines], axis=1
            )

        for h in range(kv_local * GROUP):
            value = turn(query[:, h * HD : (h + 1) * HD])
            qs[h] = value.reshape(per, tree, HD)
        for i in range(2 * kv_local):
            value = keyval[:, i * HD : (i + 1) * HD]
            if i % 2 == 0:
                value = turn(value)
            value = value.astype(BF16).astype(F32).reshape(per, tree, HD)
            kvs[pl.ds(c * per, per), i] = value

        def attend(i, inner):
            r = c * per + i
            live = positions < lengths[r]
            mask = marks[r] > 0.5
            mask = jnp.concatenate([mask.astype(F32)] * GROUP, axis=0) > 0.5
            for g in range(kv_local):
                q = qs[g * GROUP : (g + 1) * GROUP, i].reshape(GROUP * tree, HD).astype(BF16)
                low = g * 2 * HD
                keys = kept[r, low : low + HD, :]
                values = kept[r, low + HD : low + 2 * HD, :]
                tree_keys = kvs[r, 2 * g].astype(BF16)
                tree_values = kvs[r, 2 * g + 1].astype(BF16)
                a = jnp.dot(q, keys, preferred_element_type=F32) * scale
                b = lax.dot_general(
                    q, tree_keys, (((1,), (1,)), ((), ())), preferred_element_type=F32
                ) * scale
                a = jnp.where(live, a, -1e30)
                b = jnp.where(mask, b, -1e30)
                top = jnp.maximum(
                    jnp.max(a, axis=1, keepdims=True), jnp.max(b, axis=1, keepdims=True)
                )
                a, b = jnp.exp(a - top), jnp.exp(b - top)
                total = jnp.sum(a, axis=1, keepdims=True) + jnp.sum(b, axis=1, keepdims=True)
                inverse_total = 1.0 / total
                a = (a * inverse_total).astype(BF16)
                b = (b * inverse_total).astype(BF16)
                value = lax.dot_general(
                    a, values, (((1,), (1,)), ((), ())), preferred_element_type=F32
                ) + jnp.dot(b, tree_values, preferred_element_type=F32)
                for j in range(GROUP):
                    h = g * GROUP + j
                    ctx[i, :, h * HD : (h + 1) * HD] = value[j * tree : (j + 1) * tree]
            return inner

        lax.fori_loop(0, per, attend, 0, unroll=2)
        rounded = ctx[...].reshape(crows, kv_local * GROUP * HD).astype(BF16)
        for g in range(t):
            part[c, g] = jnp.dot(
                rounded, wo[:, g * width : (g + 1) * width], preferred_element_type=F32
            ).astype(BF16)

    for c in range(chunks):
        chunk(c)
        reduce_start(c)

    level_c = lax.broadcasted_iota(jnp.int32, (PAD, cache_len), 0)
    place_c = lax.broadcasted_iota(jnp.int32, (PAD, cache_len), 1)
    n_accept = accepted.shape[0]
    token = lax.broadcasted_iota(jnp.int32, (n_accept, tree), 1)
    asked = lax.broadcasted_iota(jnp.int32, accepted.shape, 1)

    def write_note(k, target):
        r = request_for(at_req(k))
        path = jnp.sum(jnp.where(asked == r, accepted[...], 0), axis=1, keepdims=True)
        pick = (token == path).astype(F32)
        pick = jnp.concatenate([pick, jnp.zeros((PAD - n_accept, tree), F32)], axis=0).astype(BF16)
        spot = jnp.logical_and(place_c == level_c + lengths[r], level_c < n_accept)
        target[k, 0:PAD, :] = spot.astype(F32).astype(BF16)
        chosen = [
            jnp.dot(pick, kvs[r, i].astype(BF16), preferred_element_type=F32)
            for i in range(2 * kv_local)
        ]
        chosen = jnp.concatenate(chosen, axis=1).astype(BF16)
        target[k, PAD : 2 * PAD, 0 : 2 * kv_local * HD] = chosen

    def note_copy(k):
        return pltpu.make_async_remote_copy(
            src_ref=note_out.at[k],
            dst_ref=note_in.at[k],
            send_sem=note_send.at[k],
            recv_sem=note_recv.at[k],
            device_id=(at_req(k), tp),
            device_id_type=MESH,
        )

    def send_note(k, carry):
        write_note(k, note_out)
        note_copy(k).start()
        return carry

    note_out[...] = jnp.zeros_like(note_out)
    lax.fori_loop(1, n, send_note, 0)
    note_in[0] = jnp.zeros_like(note_in[0])
    write_note(0, note_in)

    def out_copy(k):
        return pltpu.make_async_copy(
            landed.at[k], new_cache.at[lax.rem(req + n - k, n)], out_sem.at[k]
        )

    def finish(k):
        spot = note_in[k, 0:PAD, :]
        chosen = note_in[k, PAD : 2 * PAD, 0 : 2 * kv_local * HD]
        added = lax.dot_general(chosen, spot, (((0,), (0,)), ((), ())), preferred_element_type=F32)
        landed[k] = landed[k] + added.astype(BF16)
        out_copy(k).start()

    finish(0)
    reduce_pass(chunks - 1)

    def receive(k, carry):
        move_copy(k).wait_recv()
        note_copy(k).wait_recv()
        finish(k)
        return carry

    lax.fori_loop(1, n, receive, 0)

    for c in range(chunks):
        where = slice(c * crows, (c + 1) * crows)
        out_rows[where, :] = (reduce_sum(c, 0) + hidden[where, :].astype(F32)).astype(BF16)

    for c in range(chunks):
        for m in range(t):
            for b in strides:
                if m == 0 or b < low(m):
                    gather_copy(c, m, b).wait_send()
        for m in range(1, t):
            reduce_copy(c, m).wait_send()

    def drain(k, carry):
        move_copy(k).wait_send()
        note_copy(k).wait_send()
        out_copy(k).wait()
        return carry

    lax.fori_loop(1, n, drain, 0)
    out_copy(0).wait()


def hand_over(rows, cache, out_rows, new_cache):
    out_rows[...] = rows[...]
    new_cache[...] = cache[...]


def per_device(
    n, t,
    hidden, norm_gain, w_query, w_keyval, w_out, kv_cache, lengths, parents, accepted, slot_of
):
    requests, tree, width = hidden.shape
    rows = requests * tree
    features = w_query.shape[0]
    q_width = w_query.shape[1]
    kv_rows = w_keyval.shape[0]
    cache_len = kv_cache.shape[2]
    chunks = 2
    per = requests // chunks
    crows = per * tree
    heads = q_width // HD
    freq = jnp.asarray(
        (10000.0 ** (-2.0 * np.arange(HALF, dtype=np.float64) / HD)).astype(np.float32)
    ).reshape(1, HALF)
    smem = pl.BlockSpec(memory_space=pltpu.SMEM)
    vmem = pl.BlockSpec(memory_space=pltpu.VMEM)
    hbm = pl.BlockSpec(memory_space=pl.ANY)
    dma = pltpu.SemaphoreType.DMA
    out_rows, new_cache = pl.pallas_call(
        functools.partial(kernel, n, t, chunks, requests, tree),
        out_shape=(
            jax.ShapeDtypeStruct((rows, width), BF16),
            jax.ShapeDtypeStruct(kv_cache.shape, BF16),
        ),
        in_specs=[smem] * 2 + [vmem] * 5 + [hbm] * 4,
        out_specs=(vmem, hbm),
        scratch_shapes=[
            pltpu.VMEM(w_query.shape, BF16),
            pltpu.VMEM(w_keyval.shape, BF16),
            pltpu.VMEM(w_out.shape, BF16),
            pltpu.VMEM(kv_cache.shape, BF16),
            pltpu.VMEM((n,) + kv_cache.shape[1:], BF16),
            pltpu.VMEM((n,) + kv_cache.shape[1:], BF16),
            pltpu.VMEM((n, 2 * PAD, cache_len), BF16),
            pltpu.VMEM((n, 2 * PAD, cache_len), BF16),
            pltpu.VMEM((chunks, t, crows, width), BF16),
            pltpu.VMEM((crows, features), BF16),
            pltpu.VMEM((heads, per, tree, HD), F32),
            pltpu.VMEM((requests, kv_rows // HD, tree, HD), F32),
            pltpu.VMEM((requests, tree, tree), F32),
            pltpu.VMEM((requests, tree, 1), F32),
            pltpu.VMEM((per, tree, q_width), F32),
            pltpu.VMEM((chunks, t, crows, width), BF16),
            pltpu.VMEM((chunks, t, crows, width), BF16),
            pltpu.VMEM((chunks, t, crows, width), BF16),
            pltpu.VMEM((2, requests, tree, HALF), F32),
            dma((3,)),
            dma((requests,)),
            dma((chunks, t)),
            dma((chunks, t)),
            dma((chunks, t)),
            dma((chunks, t)),
            dma((n,)),
            dma((n,)),
            dma((n,)),
            dma((n,)),
            dma((n,)),
        ],
        compiler_params=pltpu.CompilerParams(
            collective_id=0, has_side_effects=True, vmem_limit_bytes=56 * 1024 * 1024
        ),
    )(
        lengths, slot_of, accepted.T, hidden.reshape(rows, width), norm_gain,
        freq, parents, w_query, w_keyval, w_out, kv_cache,
    )
    rows_shape, cache_shape = out_rows.shape, new_cache.shape
    rows_spec = pl.BlockSpec((2 * tree, width), lambda i: (i, 0))
    cache_spec = pl.BlockSpec((2,) + cache_shape[1:], lambda i: (i, 0, 0))
    out_rows, new_cache = pl.pallas_call(
        hand_over,
        out_shape=(
            jax.ShapeDtypeStruct(rows_shape, BF16),
            jax.ShapeDtypeStruct(cache_shape, BF16),
        ),
        grid=(requests // 2,),
        in_specs=[rows_spec, cache_spec],
        out_specs=(rows_spec, cache_spec),
        compiler_params=pltpu.CompilerParams(vmem_limit_bytes=60 * 1024 * 1024),
    )(out_rows, new_cache)
    return (out_rows.reshape(requests, tree, width), new_cache)


def solution(mesh):
    in_specs = (
        P("req", None, "tp"),
        P(),
        P(None, "tp"),
        P("tp", None),
        P("tp", None),
        P("req", "tp", None),
        P("req"),
        P("req", None),
        P("req", None),
        P("req"),
    )
    out_specs = (P("req", None, "tp"), P("req", "tp", None))
    return jax.shard_map(
        functools.partial(per_device, mesh.shape["req"], mesh.shape["tp"]),
        mesh=mesh, in_specs=in_specs, out_specs=out_specs, check_vma=False,
    )
```

```python
import functools
import math

import jax
import jax.numpy as jnp
import numpy as np
from jax import lax
from jax.experimental import pallas as pl
from jax.experimental.pallas import tpu as pltpu
from jax.sharding import PartitionSpec as P

H = 32
KVH = 8
HD = 80
HALF = HD // 2
GROUP = H // KVH
MESH = pl.DeviceIdType.MESH
F32 = jnp.float32
BF16 = jnp.bfloat16
PAD = 16
LANES = 128
TOGETHER = 2


def kernel(
    n, t, chunks, requests, tree,
    lengths, slots, accepted, hidden, gain, freq, parent, w_query, w_keyval, w_out, cache,
    out_rows, new_cache,
    wq, wkv, wo, kept, stage, landed, note_out, note_in, full, nrm, qs, kvs, marks, depth,
    ctx, part, outgoing, incoming, turns,
    w_sem, cache_sem, ag_send, ag_recv, rs_send, rs_recv, move_send, move_recv,
    note_send, note_recv, out_sem,
):
    req, tp = lax.axis_index("req"), lax.axis_index("tp")
    rows, width = hidden.shape
    per = requests // chunks
    crows = per * tree
    cache_len = cache.shape[2]
    kv_local = wkv.shape[0] // (2 * HD)
    scale = 1.0 / math.sqrt(HD)

    def at_req(k):
        return lax.rem(req + k, n)

    def at_tp(k):
        return lax.rem(tp + k, t)

    def load_cache(r, carry):
        pltpu.make_async_copy(cache.at[r], kept.at[r], cache_sem.at[r]).start()
        return carry

    lax.fori_loop(0, requests, load_cache, 0)
    loads = [
        pltpu.make_async_copy(src, dst, w_sem.at[i])
        for i, (src, dst) in enumerate(((w_query, wq), (w_keyval, wkv), (w_out, wo)))
    ]
    for copy in loads:
        copy.start()

    barrier = pltpu.get_barrier_semaphore()
    for k in range(1, n):
        pl.semaphore_signal(barrier, inc=1, device_id=(at_req(k), tp), device_id_type=MESH)

    strides = [1 << j for j in range(t.bit_length() - 1)]

    def flip(m):
        place = tp
        for b in strides:
            if m & b:
                place = place + b * (1 - 2 * lax.rem(tp // b, 2))
        return place

    for b in strides:
        pl.semaphore_signal(barrier, inc=1, device_id=(req, flip(b)), device_id_type=MESH)
    pl.semaphore_wait(barrier, n - 1 + len(strides))

    def low(m):
        return m & -m

    def gather_copy(c, m, b):
        slot = flip(m)
        return pltpu.make_async_remote_copy(
            src_ref=full.at[c, slot],
            dst_ref=full.at[c, slot],
            send_sem=ag_send.at[c, m | b],
            recv_sem=ag_recv.at[c, m | b],
            device_id=(req, flip(b)),
            device_id_type=MESH,
        )

    def gather_start(c):
        full[c, tp] = hidden[c * crows : (c + 1) * crows]
        for b in reversed(strides):
            gather_copy(c, 0, b).start()

    def gather_wait(c, m):
        slot = flip(m)
        pltpu.make_async_remote_copy(
            src_ref=full.at[c, slot],
            dst_ref=full.at[c, slot],
            send_sem=ag_send.at[c, m],
            recv_sem=ag_recv.at[c, m],
            device_id=(req, flip(low(m))),
            device_id_type=MESH,
        ).wait_recv()

    passed_on = sorted((m for m in range(2, t) if low(m) > 1), key=low, reverse=True)

    def gather_pass(c):
        for m in passed_on:
            gather_wait(c, m)
            for b in reversed(strides):
                if b < low(m):
                    gather_copy(c, m, b).start()

    def gather_end(c):
        for m in range(1, t, 2):
            gather_wait(c, m)

    for c in range(chunks):
        gather_start(c)
    gains = gain[...].reshape(1, t * width)

    positions = lax.broadcasted_iota(jnp.int32, (1, cache_len), 1)

    def request_for(dest):
        first = dest * requests
        found = jnp.int32(0)
        for r in range(1, requests):
            here = jnp.logical_and(slots[r] >= first, slots[r] < first + requests)
            found = jnp.where(here, r, found)
        return found

    def kept_only(r):
        live = jnp.where(positions < lengths[r], 1.0, 0.0)
        live = jnp.broadcast_to(live, (PAD, cache_len)).astype(BF16)
        value = kept[r]
        return (value.reshape(-1, PAD, cache_len) * live[None]).reshape(value.shape)

    def wait_cache(r, carry):
        pltpu.make_async_copy(cache.at[r], kept.at[r], cache_sem.at[r]).wait()
        return carry

    lax.fori_loop(0, requests, wait_cache, 0)

    def move_copy(k):
        return pltpu.make_async_remote_copy(
            src_ref=stage.at[k],
            dst_ref=landed.at[k],
            send_sem=move_send.at[k],
            recv_sem=move_recv.at[k],
            device_id=(at_req(k), tp),
            device_id_type=MESH,
        )

    def move(k, carry):
        r = request_for(at_req(k))
        stage[k] = kept_only(r)
        move_copy(k).start()
        return carry

    lax.fori_loop(1, n, move, 0)
    own = request_for(req)
    landed[0] = kept_only(own)

    gather_pass(0)

    seen = lax.broadcasted_iota(jnp.int32, (rows, rows), 0)
    line = lax.broadcasted_iota(jnp.int32, (rows, rows), 1)
    parent_row = jnp.concatenate(
        [parent[r : r + 1, :] + r * tree for r in range(requests)], axis=1
    )
    reach = jnp.logical_or(seen == parent_row, seen == line).astype(F32).astype(BF16)
    covered = 1
    while covered < tree:
        reach = jnp.minimum(jnp.dot(reach, reach, preferred_element_type=F32), 1.0).astype(BF16)
        covered *= 2
    fold = (
        lax.rem(lax.broadcasted_iota(jnp.int32, (rows, LANES), 0), tree)
        == lax.broadcasted_iota(jnp.int32, (rows, LANES), 1)
    ).astype(F32).astype(BF16)
    local = lax.dot_general(reach, fold, (((0,), (0,)), ((), ())), preferred_element_type=F32)
    marks[...] = local.reshape(requests, tree, LANES)
    depth[...] = (jnp.sum(local, axis=1, keepdims=True) - 1.0).reshape(requests, tree, 1)

    for r in range(requests):
        angles = (depth[r] + lengths[r].astype(F32)) * freq[...]
        turns[0, r] = jnp.cos(angles)
        turns[1, r] = jnp.sin(angles)

    for copy in loads:
        copy.wait()

    def reduce_copy(c, m):
        return pltpu.make_async_remote_copy(
            src_ref=outgoing.at[c, m],
            dst_ref=incoming.at[c, m],
            send_sem=rs_send.at[c, m],
            recv_sem=rs_recv.at[c, m],
            device_id=(req, flip(low(m))),
            device_id_type=MESH,
        )

    def reduce_sum(c, m):
        value = part[c, flip(m)].astype(F32)
        for b in strides:
            if m == 0 or b < low(m):
                reduce_copy(c, m | b).wait_recv()
                value += incoming[c, m | b].astype(F32)
        return value

    def reduce_start(c):
        for m in range(t - 1, 0, -2):
            outgoing[c, m] = part[c, flip(m)]
            reduce_copy(c, m).start()

    def reduce_pass(c):
        for m in sorted(passed_on, key=low):
            outgoing[c, m] = reduce_sum(c, m).astype(BF16)
            reduce_copy(c, m).start()

    def chunk(c):
        gather_end(c)
        spread = jnp.zeros((crows, 1), F32)
        for g in range(t):
            value = full[c, g].astype(F32)
            spread += jnp.sum(value * value, axis=1, keepdims=True)
        inverse = lax.rsqrt(spread / (t * width) + 1e-05)
        for g in range(t):
            value = full[c, g].astype(F32)
            nrm[:, g * width : (g + 1) * width] = (value * inverse * gains[:, g * width : (g + 1) * width]).astype(BF16)
        normed = nrm[...]
        query = jnp.dot(normed, wq[...], preferred_element_type=F32)
        keyval = lax.dot_general(
            normed, wkv[...], (((1,), (1,)), ((), ())), preferred_element_type=F32
        )
        if c + 1 < chunks:
            gather_pass(c + 1)
        if c > 0:
            reduce_pass(c - 1)
        cosines = turns[0, c * per : (c + 1) * per].reshape(crows, HALF)
        sines = turns[1, c * per : (c + 1) * per].reshape(crows, HALF)

        def turn(value):
            first, second = value[:, :HALF], value[:, HALF:]
            return jnp.concatenate(
                [first * cosines - second * sines, second * cosines + first * sines], axis=1
            )

        for h in range(kv_local * GROUP):
            value = turn(query[:, h * HD : (h + 1) * HD]) * scale
            qs[h] = value.reshape(per, tree, HD)
        for i in range(2 * kv_local):
            value = keyval[:, i * HD : (i + 1) * HD]
            if i % 2 == 0:
                value = turn(value)
            value = value.astype(BF16).astype(F32).reshape(per, tree, HD)
            kvs[pl.ds(c * per, per), i] = value

        def attend(pair, inner):
            jobs = [(pair * TOGETHER + u, g) for u in range(TOGETHER) for g in range(kv_local)]
            scores = []
            for i, g in jobs:
                r = c * per + i
                q = qs[g * GROUP : (g + 1) * GROUP, i].reshape(GROUP * tree, HD).astype(BF16)
                tree_keys = jnp.concatenate([kvs[r, 2 * g], blank], axis=0).astype(BF16)
                keys = kept[r, g * 2 * HD : g * 2 * HD + HD, :]
                a = jnp.dot(q, keys, preferred_element_type=F32)
                b = lax.dot_general(
                    q, tree_keys, (((1,), (1,)), ((), ())), preferred_element_type=F32
                )
                scores.append((a, b))
            weights = []
            for (i, g), (a, b) in zip(jobs, scores):
                r = c * per + i
                mask = jnp.concatenate([marks[r]] * GROUP, axis=0) > 0.5
                both = jnp.concatenate(
                    [jnp.where(positions < lengths[r], a, -1e30), jnp.where(mask, b, -1e30)], axis=1
                )
                both = jnp.exp(both - jnp.max(both, axis=1, keepdims=True))
                weights.append((both.astype(BF16), jnp.sum(both, axis=1, keepdims=True)))
            results = []
            for (i, g), (both, total) in zip(jobs, weights):
                r = c * per + i
                values = kept[r, g * 2 * HD + HD : (g + 1) * 2 * HD, :]
                tree_values = jnp.concatenate([kvs[r, 2 * g + 1], blank], axis=0).astype(BF16)
                value = lax.dot_general(
                    both[:, :cache_len], values, (((1,), (1,)), ((), ())),
                    preferred_element_type=F32,
                ) + jnp.dot(both[:, cache_len:], tree_values, preferred_element_type=F32)
                results.append(value / total)
            for (i, g), value in zip(jobs, results):
                for j in range(GROUP):
                    h = g * GROUP + j
                    ctx[i, :, h * HD : (h + 1) * HD] = value[j * tree : (j + 1) * tree]
            return inner

        lax.fori_loop(0, per // TOGETHER, attend, 0)
        rounded = ctx[...].reshape(crows, kv_local * GROUP * HD).astype(BF16)
        for g in range(t):
            part[c, g] = jnp.dot(
                rounded, wo[:, g * width : (g + 1) * width], preferred_element_type=F32
            ).astype(BF16)

    blank = jnp.zeros((LANES - tree, HD), F32)
    for c in range(chunks):
        chunk(c)
        reduce_start(c)

    level_c = lax.broadcasted_iota(jnp.int32, (PAD, cache_len), 0)
    place_c = lax.broadcasted_iota(jnp.int32, (PAD, cache_len), 1)
    n_accept = accepted.shape[0]
    token = lax.broadcasted_iota(jnp.int32, (n_accept, tree), 1)
    asked = lax.broadcasted_iota(jnp.int32, accepted.shape, 1)

    def write_note(k, target):
        r = request_for(at_req(k))
        path = jnp.sum(jnp.where(asked == r, accepted[...], 0), axis=1, keepdims=True)
        pick = (token == path).astype(F32)
        pick = jnp.concatenate([pick, jnp.zeros((PAD - n_accept, tree), F32)], axis=0).astype(BF16)
        spot = jnp.logical_and(place_c == level_c + lengths[r], level_c < n_accept)
        target[k, 0:PAD, :] = spot.astype(F32).astype(BF16)
        chosen = [
            jnp.dot(pick, kvs[r, i].astype(BF16), preferred_element_type=F32)
            for i in range(2 * kv_local)
        ]
        chosen = jnp.concatenate(chosen, axis=1).astype(BF16)
        target[k, PAD : 2 * PAD, 0 : 2 * kv_local * HD] = chosen

    def note_copy(k):
        return pltpu.make_async_remote_copy(
            src_ref=note_out.at[k],
            dst_ref=note_in.at[k],
            send_sem=note_send.at[k],
            recv_sem=note_recv.at[k],
            device_id=(at_req(k), tp),
            device_id_type=MESH,
        )

    def send_note(k, carry):
        write_note(k, note_out)
        note_copy(k).start()
        return carry

    note_out[...] = jnp.zeros_like(note_out)
    lax.fori_loop(1, n, send_note, 0)
    note_in[0] = jnp.zeros_like(note_in[0])
    write_note(0, note_in)

    def out_copy(k):
        return pltpu.make_async_copy(
            landed.at[k], new_cache.at[lax.rem(req + n - k, n)], out_sem.at[k]
        )

    def finish(k):
        spot = note_in[k, 0:PAD, :]
        chosen = note_in[k, PAD : 2 * PAD, 0 : 2 * kv_local * HD]
        added = lax.dot_general(chosen, spot, (((0,), (0,)), ((), ())), preferred_element_type=F32)
        landed[k] = landed[k] + added.astype(BF16)
        out_copy(k).start()

    finish(0)
    reduce_pass(chunks - 1)

    def receive(k, carry):
        move_copy(k).wait_recv()
        note_copy(k).wait_recv()
        finish(k)
        return carry

    lax.fori_loop(1, n, receive, 0)

    for c in range(chunks):
        where = slice(c * crows, (c + 1) * crows)
        out_rows[where, :] = (reduce_sum(c, 0) + hidden[where, :].astype(F32)).astype(BF16)

    for c in range(chunks):
        for m in range(t):
            for b in strides:
                if m == 0 or b < low(m):
                    gather_copy(c, m, b).wait_send()
        for m in range(1, t):
            reduce_copy(c, m).wait_send()

    def drain(k, carry):
        move_copy(k).wait_send()
        note_copy(k).wait_send()
        out_copy(k).wait()
        return carry

    lax.fori_loop(1, n, drain, 0)
    out_copy(0).wait()


def hand_over(rows, cache, out_rows, new_cache, rows_held, held, in_sem, out_sem):
    count = cache.shape[0]
    moves = [(cache.at[i], held.at[i], new_cache.at[i]) for i in range(count)]
    moves.append((rows, rows_held, out_rows))
    first = [pltpu.make_async_copy(m[0], m[1], in_sem.at[i]) for i, m in enumerate(moves)]
    second = [pltpu.make_async_copy(m[1], m[2], out_sem.at[i]) for i, m in enumerate(moves)]
    for copy in first:
        copy.start()
    for copy, after in zip(first, second):
        copy.wait()
        after.start()
    for copy in second:
        copy.wait()


def per_device(
    n, t,
    hidden, norm_gain, w_query, w_keyval, w_out, kv_cache, lengths, parents, accepted, slot_of
):
    requests, tree, width = hidden.shape
    rows = requests * tree
    features = w_query.shape[0]
    q_width = w_query.shape[1]
    kv_rows = w_keyval.shape[0]
    cache_len = kv_cache.shape[2]
    chunks = 2
    per = requests // chunks
    crows = per * tree
    heads = q_width // HD
    freq = jnp.asarray(
        (10000.0 ** (-2.0 * np.arange(HALF, dtype=np.float64) / HD)).astype(np.float32)
    ).reshape(1, HALF)
    smem = pl.BlockSpec(memory_space=pltpu.SMEM)
    vmem = pl.BlockSpec(memory_space=pltpu.VMEM)
    hbm = pl.BlockSpec(memory_space=pl.ANY)
    dma = pltpu.SemaphoreType.DMA
    out_rows, new_cache = pl.pallas_call(
        functools.partial(kernel, n, t, chunks, requests, tree),
        out_shape=(
            jax.ShapeDtypeStruct((rows, width), BF16),
            jax.ShapeDtypeStruct(kv_cache.shape, BF16),
        ),
        in_specs=[smem] * 2 + [vmem] * 5 + [hbm] * 4,
        out_specs=(vmem, hbm),
        scratch_shapes=[
            pltpu.VMEM(w_query.shape, BF16),
            pltpu.VMEM(w_keyval.shape, BF16),
            pltpu.VMEM(w_out.shape, BF16),
            pltpu.VMEM(kv_cache.shape, BF16),
            pltpu.VMEM((n,) + kv_cache.shape[1:], BF16),
            pltpu.VMEM((n,) + kv_cache.shape[1:], BF16),
            pltpu.VMEM((n, 2 * PAD, cache_len), BF16),
            pltpu.VMEM((n, 2 * PAD, cache_len), BF16),
            pltpu.VMEM((chunks, t, crows, width), BF16),
            pltpu.VMEM((crows, features), BF16),
            pltpu.VMEM((heads, per, tree, HD), F32),
            pltpu.VMEM((requests, kv_rows // HD, tree, HD), F32),
            pltpu.VMEM((requests, tree, LANES), F32),
            pltpu.VMEM((requests, tree, 1), F32),
            pltpu.VMEM((per, tree, q_width), F32),
            pltpu.VMEM((chunks, t, crows, width), BF16),
            pltpu.VMEM((chunks, t, crows, width), BF16),
            pltpu.VMEM((chunks, t, crows, width), BF16),
            pltpu.VMEM((2, requests, tree, HALF), F32),
            dma((3,)),
            dma((requests,)),
            dma((chunks, t)),
            dma((chunks, t)),
            dma((chunks, t)),
            dma((chunks, t)),
            dma((n,)),
            dma((n,)),
            dma((n,)),
            dma((n,)),
            dma((n,)),
        ],
        compiler_params=pltpu.CompilerParams(
            collective_id=0, has_side_effects=True, vmem_limit_bytes=56 * 1024 * 1024
        ),
    )(
        lengths, slot_of, accepted.T, hidden.reshape(rows, width), norm_gain,
        freq, parents, w_query, w_keyval, w_out, kv_cache,
    )
    rows_shape, cache_shape = out_rows.shape, new_cache.shape
    out_rows, new_cache = pl.pallas_call(
        hand_over,
        out_shape=(
            jax.ShapeDtypeStruct(rows_shape, BF16),
            jax.ShapeDtypeStruct(cache_shape, BF16),
        ),
        in_specs=[hbm, hbm],
        out_specs=(hbm, hbm),
        scratch_shapes=[
            pltpu.VMEM(rows_shape, BF16),
            pltpu.VMEM(cache_shape, BF16),
            dma((cache_shape[0] + 1,)),
            dma((cache_shape[0] + 1,)),
        ],
        compiler_params=pltpu.CompilerParams(vmem_limit_bytes=60 * 1024 * 1024),
    )(out_rows, new_cache)
    return (out_rows.reshape(requests, tree, width), new_cache)


def solution(mesh):
    in_specs = (
        P("req", None, "tp"),
        P(),
        P(None, "tp"),
        P("tp", None),
        P("tp", None),
        P("req", "tp", None),
        P("req"),
        P("req", None),
        P("req", None),
        P("req"),
    )
    out_specs = (P("req", None, "tp"), P("req", "tp", None))
    return jax.shard_map(
        functools.partial(per_device, mesh.shape["req"], mesh.shape["tp"]),
        mesh=mesh, in_specs=in_specs, out_specs=out_specs, check_vma=False,
    )
```

```python
import functools
import math

import jax
import jax.numpy as jnp
import numpy as np
from jax import lax
from jax.experimental import pallas as pl
from jax.experimental.pallas import tpu as pltpu
from jax.sharding import PartitionSpec as P

H = 32
KVH = 8
HD = 80
HALF = HD // 2
GROUP = H // KVH
MESH = pl.DeviceIdType.MESH
F32 = jnp.float32
BF16 = jnp.bfloat16
PAD = 16
LANES = 128
TOGETHER = 2


def kernel(
    n, t, chunks, requests, tree,
    lengths, slots, accepted, hidden, gain, freq, parent, w_query, w_keyval, w_out, cache,
    out_rows, new_cache,
    wq, wkv, wo, kept, stage, landed, note_out, note_in, full, nrm, qs, kvs, marks, depth,
    ctx, part, outgoing, incoming, turns,
    w_sem, cache_sem, ag_send, ag_recv, rs_send, rs_recv, move_send, move_recv,
    note_send, note_recv, out_sem,
):
    req, tp = lax.axis_index("req"), lax.axis_index("tp")
    rows, width = hidden.shape
    per = requests // chunks
    crows = per * tree
    cache_len = cache.shape[2]
    kv_local = wkv.shape[0] // (2 * HD)
    scale = 1.0 / math.sqrt(HD)

    def at_req(k):
        return lax.rem(req + k, n)

    def at_tp(k):
        return lax.rem(tp + k, t)

    def load_cache(r, carry):
        pltpu.make_async_copy(cache.at[r], kept.at[r], cache_sem.at[r]).start()
        return carry

    lax.fori_loop(0, requests, load_cache, 0)
    loads = [
        pltpu.make_async_copy(src, dst, w_sem.at[i])
        for i, (src, dst) in enumerate(((w_query, wq), (w_keyval, wkv), (w_out, wo)))
    ]
    for copy in loads:
        copy.start()

    barrier = pltpu.get_barrier_semaphore()
    for k in range(1, n):
        pl.semaphore_signal(barrier, inc=1, device_id=(at_req(k), tp), device_id_type=MESH)

    strides = [1 << j for j in range(t.bit_length() - 1)]

    def flip(m):
        place = tp
        for b in strides:
            if m & b:
                place = place + b * (1 - 2 * lax.rem(tp // b, 2))
        return place

    for b in strides:
        pl.semaphore_signal(barrier, inc=1, device_id=(req, flip(b)), device_id_type=MESH)
    positions = lax.broadcasted_iota(jnp.int32, (1, cache_len), 1)

    def request_for(dest):
        first = dest * requests
        found = jnp.int32(0)
        for r in range(1, requests):
            here = jnp.logical_and(slots[r] >= first, slots[r] < first + requests)
            found = jnp.where(here, r, found)
        return found

    def kept_only(r):
        live = jnp.where(positions < lengths[r], 1.0, 0.0)
        live = jnp.broadcast_to(live, (PAD, cache_len)).astype(BF16)
        value = kept[r]
        return (value.reshape(-1, PAD, cache_len) * live[None]).reshape(value.shape)

    def wait_cache(r, carry):
        pltpu.make_async_copy(cache.at[r], kept.at[r], cache_sem.at[r]).wait()
        return carry

    lax.fori_loop(0, requests, wait_cache, 0)

    def put(k, carry):
        stage[k] = kept_only(request_for(at_req(k)))
        return carry

    lax.fori_loop(1, n, put, 0)

    pl.semaphore_wait(barrier, n - 1 + len(strides))

    def low(m):
        return m & -m

    def gather_copy(c, m, b):
        slot = flip(m)
        return pltpu.make_async_remote_copy(
            src_ref=full.at[c, slot],
            dst_ref=full.at[c, slot],
            send_sem=ag_send.at[c, m | b],
            recv_sem=ag_recv.at[c, m | b],
            device_id=(req, flip(b)),
            device_id_type=MESH,
        )

    def gather_start(c):
        full[c, tp] = hidden[c * crows : (c + 1) * crows]
        for b in reversed(strides):
            gather_copy(c, 0, b).start()

    def gather_wait(c, m):
        slot = flip(m)
        pltpu.make_async_remote_copy(
            src_ref=full.at[c, slot],
            dst_ref=full.at[c, slot],
            send_sem=ag_send.at[c, m],
            recv_sem=ag_recv.at[c, m],
            device_id=(req, flip(low(m))),
            device_id_type=MESH,
        ).wait_recv()

    passed_on = sorted((m for m in range(2, t) if low(m) > 1), key=low, reverse=True)

    def gather_pass(c):
        for m in passed_on:
            gather_wait(c, m)
            for b in reversed(strides):
                if b < low(m):
                    gather_copy(c, m, b).start()

    def gather_end(c):
        for m in range(1, t, 2):
            gather_wait(c, m)

    for c in range(chunks):
        gather_start(c)
    gains = gain[...].reshape(1, t * width)

    def move_copy(k):
        return pltpu.make_async_remote_copy(
            src_ref=stage.at[k],
            dst_ref=landed.at[k],
            send_sem=move_send.at[k],
            recv_sem=move_recv.at[k],
            device_id=(at_req(k), tp),
            device_id_type=MESH,
        )

    def move(k, carry):
        move_copy(k).start()
        return carry

    lax.fori_loop(1, n, move, 0)
    landed[0] = kept_only(request_for(req))

    seen = lax.broadcasted_iota(jnp.int32, (rows, rows), 0)
    line = lax.broadcasted_iota(jnp.int32, (rows, rows), 1)
    parent_row = jnp.concatenate(
        [parent[r : r + 1, :] + r * tree for r in range(requests)], axis=1
    )
    reach = jnp.logical_or(seen == parent_row, seen == line).astype(F32).astype(BF16)
    covered = 1
    while covered < tree:
        reach = jnp.minimum(jnp.dot(reach, reach, preferred_element_type=F32), 1.0).astype(BF16)
        covered *= 2
    fold = (
        lax.rem(lax.broadcasted_iota(jnp.int32, (rows, LANES), 0), tree)
        == lax.broadcasted_iota(jnp.int32, (rows, LANES), 1)
    ).astype(F32).astype(BF16)
    local = lax.dot_general(reach, fold, (((0,), (0,)), ((), ())), preferred_element_type=F32)
    marks[...] = local.reshape(requests, tree, LANES)
    depth[...] = (jnp.sum(local, axis=1, keepdims=True) - 1.0).reshape(requests, tree, 1)

    gather_pass(0)

    for r in range(requests):
        angles = (depth[r] + lengths[r].astype(F32)) * freq[...]
        turns[0, r] = jnp.cos(angles)
        turns[1, r] = jnp.sin(angles)

    for copy in loads:
        copy.wait()

    def reduce_copy(c, m):
        return pltpu.make_async_remote_copy(
            src_ref=outgoing.at[c, m],
            dst_ref=incoming.at[c, m],
            send_sem=rs_send.at[c, m],
            recv_sem=rs_recv.at[c, m],
            device_id=(req, flip(low(m))),
            device_id_type=MESH,
        )

    def reduce_sum(c, m):
        value = part[c, flip(m)].astype(F32)
        for b in strides:
            if m == 0 or b < low(m):
                reduce_copy(c, m | b).wait_recv()
                value += incoming[c, m | b].astype(F32)
        return value

    def reduce_start(c):
        for m in range(t - 1, 0, -2):
            outgoing[c, m] = part[c, flip(m)]
            reduce_copy(c, m).start()

    def reduce_pass(c):
        for m in sorted(passed_on, key=low):
            outgoing[c, m] = reduce_sum(c, m).astype(BF16)
            reduce_copy(c, m).start()

    def chunk(c):
        gather_end(c)
        spread = jnp.zeros((crows, 1), F32)
        for g in range(t):
            value = full[c, g].astype(F32)
            spread += jnp.sum(value * value, axis=1, keepdims=True)
        inverse = lax.rsqrt(spread / (t * width) + 1e-05)
        for g in range(t):
            value = full[c, g].astype(F32)
            nrm[:, g * width : (g + 1) * width] = (value * inverse * gains[:, g * width : (g + 1) * width]).astype(BF16)
        normed = nrm[...]
        query = jnp.dot(normed, wq[...], preferred_element_type=F32)
        keyval = lax.dot_general(
            normed, wkv[...], (((1,), (1,)), ((), ())), preferred_element_type=F32
        )
        if c + 1 < chunks:
            gather_pass(c + 1)
        if c > 0:
            reduce_pass(c - 1)
        cosines = turns[0, c * per : (c + 1) * per].reshape(crows, HALF)
        sines = turns[1, c * per : (c + 1) * per].reshape(crows, HALF)

        def turn(value):
            first, second = value[:, :HALF], value[:, HALF:]
            return jnp.concatenate(
                [first * cosines - second * sines, second * cosines + first * sines], axis=1
            )

        for h in range(kv_local * GROUP):
            value = turn(query[:, h * HD : (h + 1) * HD]) * scale
            qs[h] = value.reshape(per, tree, HD)
        for i in range(2 * kv_local):
            value = keyval[:, i * HD : (i + 1) * HD]
            if i % 2 == 0:
                value = turn(value)
            value = value.astype(BF16).astype(F32).reshape(per, tree, HD)
            kvs[pl.ds(c * per, per), i] = value

        def attend(pair, inner):
            jobs = [(pair * TOGETHER + u, g) for u in range(TOGETHER) for g in range(kv_local)]
            scores = []
            for i, g in jobs:
                r = c * per + i
                q = qs[g * GROUP : (g + 1) * GROUP, i].reshape(GROUP * tree, HD).astype(BF16)
                tree_keys = jnp.concatenate([kvs[r, 2 * g], blank], axis=0).astype(BF16)
                keys = kept[r, g * 2 * HD : g * 2 * HD + HD, :]
                a = jnp.dot(q, keys, preferred_element_type=F32)
                b = lax.dot_general(
                    q, tree_keys, (((1,), (1,)), ((), ())), preferred_element_type=F32
                )
                scores.append((a, b))
            weights = []
            for (i, g), (a, b) in zip(jobs, scores):
                r = c * per + i
                mask = jnp.concatenate([marks[r]] * GROUP, axis=0) > 0.5
                both = jnp.concatenate(
                    [jnp.where(positions < lengths[r], a, -1e30), jnp.where(mask, b, -1e30)], axis=1
                )
                both = jnp.exp(both - jnp.max(both, axis=1, keepdims=True))
                weights.append((both.astype(BF16), jnp.sum(both, axis=1, keepdims=True)))
            results = []
            for (i, g), (both, total) in zip(jobs, weights):
                r = c * per + i
                values = kept[r, g * 2 * HD + HD : (g + 1) * 2 * HD, :]
                tree_values = jnp.concatenate([kvs[r, 2 * g + 1], blank], axis=0).astype(BF16)
                value = lax.dot_general(
                    both[:, :cache_len], values, (((1,), (1,)), ((), ())),
                    preferred_element_type=F32,
                ) + jnp.dot(both[:, cache_len:], tree_values, preferred_element_type=F32)
                results.append(value / total)
            for (i, g), value in zip(jobs, results):
                for j in range(GROUP):
                    h = g * GROUP + j
                    ctx[i, :, h * HD : (h + 1) * HD] = value[j * tree : (j + 1) * tree]
            return inner

        lax.fori_loop(0, per // TOGETHER, attend, 0)
        rounded = ctx[...].reshape(crows, kv_local * GROUP * HD).astype(BF16)
        for g in range(t):
            part[c, g] = jnp.dot(
                rounded, wo[:, g * width : (g + 1) * width], preferred_element_type=F32
            ).astype(BF16)

    blank = jnp.zeros((LANES - tree, HD), F32)
    for c in range(chunks):
        chunk(c)
        reduce_start(c)

    level_c = lax.broadcasted_iota(jnp.int32, (PAD, cache_len), 0)
    place_c = lax.broadcasted_iota(jnp.int32, (PAD, cache_len), 1)
    n_accept = accepted.shape[0]
    token = lax.broadcasted_iota(jnp.int32, (n_accept, tree), 1)
    asked = lax.broadcasted_iota(jnp.int32, accepted.shape, 1)

    def write_note(k, target):
        r = request_for(at_req(k))
        path = jnp.sum(jnp.where(asked == r, accepted[...], 0), axis=1, keepdims=True)
        pick = (token == path).astype(F32)
        pick = jnp.concatenate([pick, jnp.zeros((PAD - n_accept, tree), F32)], axis=0).astype(BF16)
        spot = jnp.logical_and(place_c == level_c + lengths[r], level_c < n_accept)
        target[k, 0:PAD, :] = spot.astype(F32).astype(BF16)
        chosen = [
            jnp.dot(pick, kvs[r, i].astype(BF16), preferred_element_type=F32)
            for i in range(2 * kv_local)
        ]
        chosen = jnp.concatenate(chosen, axis=1).astype(BF16)
        target[k, PAD : 2 * PAD, 0 : 2 * kv_local * HD] = chosen

    def note_copy(k):
        return pltpu.make_async_remote_copy(
            src_ref=note_out.at[k],
            dst_ref=note_in.at[k],
            send_sem=note_send.at[k],
            recv_sem=note_recv.at[k],
            device_id=(at_req(k), tp),
            device_id_type=MESH,
        )

    def send_note(k, carry):
        write_note(k, note_out)
        note_copy(k).start()
        return carry

    note_out[...] = jnp.zeros_like(note_out)
    lax.fori_loop(1, n, send_note, 0)
    note_in[0] = jnp.zeros_like(note_in[0])
    write_note(0, note_in)

    def out_copy(k):
        return pltpu.make_async_copy(
            landed.at[k], new_cache.at[lax.rem(req + n - k, n)], out_sem.at[k]
        )

    def finish(k):
        spot = note_in[k, 0:PAD, :]
        chosen = note_in[k, PAD : 2 * PAD, 0 : 2 * kv_local * HD]
        added = lax.dot_general(chosen, spot, (((0,), (0,)), ((), ())), preferred_element_type=F32)
        landed[k] = landed[k] + added.astype(BF16)
        out_copy(k).start()

    finish(0)
    reduce_pass(chunks - 1)

    def receive(k, carry):
        move_copy(k).wait_recv()
        note_copy(k).wait_recv()
        finish(k)
        return carry

    lax.fori_loop(1, n, receive, 0)

    for c in range(chunks):
        where = slice(c * crows, (c + 1) * crows)
        out_rows[where, :] = (reduce_sum(c, 0) + hidden[where, :].astype(F32)).astype(BF16)

    for c in range(chunks):
        for m in range(t):
            for b in strides:
                if m == 0 or b < low(m):
                    gather_copy(c, m, b).wait_send()
        for m in range(1, t):
            reduce_copy(c, m).wait_send()

    def drain(k, carry):
        move_copy(k).wait_send()
        note_copy(k).wait_send()
        out_copy(k).wait()
        return carry

    lax.fori_loop(1, n, drain, 0)
    out_copy(0).wait()


def hand_over(rows, cache, out_rows, new_cache, rows_held, held, in_sem, out_sem):
    count = cache.shape[0]
    moves = [(cache.at[i], held.at[i], new_cache.at[i]) for i in range(count)]
    moves.append((rows, rows_held, out_rows))
    first = [pltpu.make_async_copy(m[0], m[1], in_sem.at[i]) for i, m in enumerate(moves)]
    second = [pltpu.make_async_copy(m[1], m[2], out_sem.at[i]) for i, m in enumerate(moves)]
    for copy in first:
        copy.start()
    for copy, after in zip(first, second):
        copy.wait()
        after.start()
    for copy in second:
        copy.wait()


def per_device(
    n, t,
    hidden, norm_gain, w_query, w_keyval, w_out, kv_cache, lengths, parents, accepted, slot_of
):
    requests, tree, width = hidden.shape
    rows = requests * tree
    features = w_query.shape[0]
    q_width = w_query.shape[1]
    kv_rows = w_keyval.shape[0]
    cache_len = kv_cache.shape[2]
    chunks = 2
    per = requests // chunks
    crows = per * tree
    heads = q_width // HD
    freq = jnp.asarray(
        (10000.0 ** (-2.0 * np.arange(HALF, dtype=np.float64) / HD)).astype(np.float32)
    ).reshape(1, HALF)
    smem = pl.BlockSpec(memory_space=pltpu.SMEM)
    vmem = pl.BlockSpec(memory_space=pltpu.VMEM)
    hbm = pl.BlockSpec(memory_space=pl.ANY)
    dma = pltpu.SemaphoreType.DMA
    out_rows, new_cache = pl.pallas_call(
        functools.partial(kernel, n, t, chunks, requests, tree),
        out_shape=(
            jax.ShapeDtypeStruct((rows, width), BF16),
            jax.ShapeDtypeStruct(kv_cache.shape, BF16),
        ),
        in_specs=[smem] * 2 + [vmem] * 5 + [hbm] * 4,
        out_specs=(vmem, hbm),
        scratch_shapes=[
            pltpu.VMEM(w_query.shape, BF16),
            pltpu.VMEM(w_keyval.shape, BF16),
            pltpu.VMEM(w_out.shape, BF16),
            pltpu.VMEM(kv_cache.shape, BF16),
            pltpu.VMEM((n,) + kv_cache.shape[1:], BF16),
            pltpu.VMEM((n,) + kv_cache.shape[1:], BF16),
            pltpu.VMEM((n, 2 * PAD, cache_len), BF16),
            pltpu.VMEM((n, 2 * PAD, cache_len), BF16),
            pltpu.VMEM((chunks, t, crows, width), BF16),
            pltpu.VMEM((crows, features), BF16),
            pltpu.VMEM((heads, per, tree, HD), F32),
            pltpu.VMEM((requests, kv_rows // HD, tree, HD), F32),
            pltpu.VMEM((requests, tree, LANES), F32),
            pltpu.VMEM((requests, tree, 1), F32),
            pltpu.VMEM((per, tree, q_width), F32),
            pltpu.VMEM((chunks, t, crows, width), BF16),
            pltpu.VMEM((chunks, t, crows, width), BF16),
            pltpu.VMEM((chunks, t, crows, width), BF16),
            pltpu.VMEM((2, requests, tree, HALF), F32),
            dma((3,)),
            dma((requests,)),
            dma((chunks, t)),
            dma((chunks, t)),
            dma((chunks, t)),
            dma((chunks, t)),
            dma((n,)),
            dma((n,)),
            dma((n,)),
            dma((n,)),
            dma((n,)),
        ],
        compiler_params=pltpu.CompilerParams(
            collective_id=0, has_side_effects=True, vmem_limit_bytes=56 * 1024 * 1024
        ),
    )(
        lengths, slot_of, accepted.T, hidden.reshape(rows, width), norm_gain,
        freq, parents, w_query, w_keyval, w_out, kv_cache,
    )
    rows_shape, cache_shape = out_rows.shape, new_cache.shape
    out_rows, new_cache = pl.pallas_call(
        hand_over,
        out_shape=(
            jax.ShapeDtypeStruct(rows_shape, BF16),
            jax.ShapeDtypeStruct(cache_shape, BF16),
        ),
        in_specs=[hbm, hbm],
        out_specs=(hbm, hbm),
        scratch_shapes=[
            pltpu.VMEM(rows_shape, BF16),
            pltpu.VMEM(cache_shape, BF16),
            dma((cache_shape[0] + 1,)),
            dma((cache_shape[0] + 1,)),
        ],
        compiler_params=pltpu.CompilerParams(vmem_limit_bytes=60 * 1024 * 1024),
    )(out_rows, new_cache)
    return (out_rows.reshape(requests, tree, width), new_cache)


def solution(mesh):
    in_specs = (
        P("req", None, "tp"),
        P(),
        P(None, "tp"),
        P("tp", None),
        P("tp", None),
        P("req", "tp", None),
        P("req"),
        P("req", None),
        P("req", None),
        P("req"),
    )
    out_specs = (P("req", None, "tp"), P("req", "tp", None))
    return jax.shard_map(
        functools.partial(per_device, mesh.shape["req"], mesh.shape["tp"]),
        mesh=mesh, in_specs=in_specs, out_specs=out_specs, check_vma=False,
    )
```

```python
import functools
import math

import jax
import jax.numpy as jnp
import numpy as np
from jax import lax
from jax.experimental import pallas as pl
from jax.experimental.pallas import tpu as pltpu
from jax.sharding import PartitionSpec as P

H = 32
KVH = 8
HD = 80
HALF = HD // 2
GROUP = H // KVH
MESH = pl.DeviceIdType.MESH
F32 = jnp.float32
BF16 = jnp.bfloat16
PAD = 16
LANES = 128
TOGETHER = 2


def kernel(
    n, t, chunks, requests, tree,
    lengths, slots, accepted, hidden, gain, freq, parent, w_query, w_keyval, w_out, cache,
    out_rows, new_cache,
    wq, wkv, wo, kept, stage, landed, note_out, note_in, full, nrm, qs, kvs, marks, depth,
    ctx, part, outgoing, incoming, turns,
    w_sem, cache_sem, ag_send, ag_recv, rs_send, rs_recv, move_send, move_recv,
    note_send, note_recv, out_sem,
):
    req, tp = lax.axis_index("req"), lax.axis_index("tp")
    rows, width = hidden.shape
    per = requests // chunks
    crows = per * tree
    cache_len = cache.shape[2]
    kv_local = wkv.shape[0] // (2 * HD)
    scale = 1.0 / math.sqrt(HD)

    def at_req(k):
        return lax.rem(req + k, n)

    def at_tp(k):
        return lax.rem(tp + k, t)

    def load_cache(r, carry):
        pltpu.make_async_copy(cache.at[r], kept.at[r], cache_sem.at[r]).start()
        return carry

    lax.fori_loop(0, requests, load_cache, 0)
    loads = [
        pltpu.make_async_copy(src, dst, w_sem.at[i])
        for i, (src, dst) in enumerate(((w_query, wq), (w_keyval, wkv), (w_out, wo)))
    ]
    for copy in loads:
        copy.start()

    barrier = pltpu.get_barrier_semaphore()
    for k in range(1, n):
        pl.semaphore_signal(barrier, inc=1, device_id=(at_req(k), tp), device_id_type=MESH)

    strides = [1 << j for j in range(t.bit_length() - 1)]

    def flip(m):
        place = tp
        for b in strides:
            if m & b:
                place = place + b * (1 - 2 * lax.rem(tp // b, 2))
        return place

    for b in strides:
        pl.semaphore_signal(barrier, inc=1, device_id=(req, flip(b)), device_id_type=MESH)
    positions = lax.broadcasted_iota(jnp.int32, (1, cache_len), 1)

    def request_for(dest):
        first = dest * requests
        found = jnp.int32(0)
        for r in range(1, requests):
            here = jnp.logical_and(slots[r] >= first, slots[r] < first + requests)
            found = jnp.where(here, r, found)
        return found

    def kept_only(r):
        live = jnp.where(positions < lengths[r], 1.0, 0.0)
        live = jnp.broadcast_to(live, (PAD, cache_len)).astype(BF16)
        value = kept[r]
        return (value.reshape(-1, PAD, cache_len) * live[None]).reshape(value.shape)

    def wait_cache(r, carry):
        pltpu.make_async_copy(cache.at[r], kept.at[r], cache_sem.at[r]).wait()
        return carry

    lax.fori_loop(0, requests, wait_cache, 0)

    def put(k, carry):
        stage[k] = kept_only(request_for(at_req(k)))
        return carry

    lax.fori_loop(1, n, put, 0)

    pl.semaphore_wait(barrier, n - 1 + len(strides))

    def low(m):
        return m & -m

    def gather_copy(c, m, b):
        slot = flip(m)
        return pltpu.make_async_remote_copy(
            src_ref=full.at[c, slot],
            dst_ref=full.at[c, slot],
            send_sem=ag_send.at[c, m | b],
            recv_sem=ag_recv.at[c, m | b],
            device_id=(req, flip(b)),
            device_id_type=MESH,
        )

    def gather_start(c):
        full[c, tp] = hidden[c * crows : (c + 1) * crows]
        for b in reversed(strides):
            gather_copy(c, 0, b).start()

    def gather_wait(c, m):
        slot = flip(m)
        pltpu.make_async_remote_copy(
            src_ref=full.at[c, slot],
            dst_ref=full.at[c, slot],
            send_sem=ag_send.at[c, m],
            recv_sem=ag_recv.at[c, m],
            device_id=(req, flip(low(m))),
            device_id_type=MESH,
        ).wait_recv()

    passed_on = sorted((m for m in range(2, t) if low(m) > 1), key=low, reverse=True)

    def gather_pass(c):
        for m in passed_on:
            gather_wait(c, m)
            for b in reversed(strides):
                if b < low(m):
                    gather_copy(c, m, b).start()
        if c + 1 < chunks:
            gather_start(c + 1)

    def gather_end(c):
        for m in range(1, t, 2):
            gather_wait(c, m)

    gather_start(0)
    gains = gain[...].reshape(1, t * width)

    def move_copy(k):
        return pltpu.make_async_remote_copy(
            src_ref=stage.at[k],
            dst_ref=landed.at[k],
            send_sem=move_send.at[k],
            recv_sem=move_recv.at[k],
            device_id=(at_req(k), tp),
            device_id_type=MESH,
        )

    def move(k, carry):
        move_copy(k).start()
        return carry

    lax.fori_loop(1, n, move, 0)
    landed[0] = kept_only(request_for(req))

    seen = lax.broadcasted_iota(jnp.int32, (rows, rows), 0)
    line = lax.broadcasted_iota(jnp.int32, (rows, rows), 1)
    parent_row = jnp.concatenate(
        [parent[r : r + 1, :] + r * tree for r in range(requests)], axis=1
    )
    reach = jnp.logical_or(seen == parent_row, seen == line).astype(F32).astype(BF16)
    covered = 1
    while covered < tree:
        reach = jnp.minimum(jnp.dot(reach, reach, preferred_element_type=F32), 1.0).astype(BF16)
        covered *= 2
    fold = (
        lax.rem(lax.broadcasted_iota(jnp.int32, (rows, LANES), 0), tree)
        == lax.broadcasted_iota(jnp.int32, (rows, LANES), 1)
    ).astype(F32).astype(BF16)
    local = lax.dot_general(reach, fold, (((0,), (0,)), ((), ())), preferred_element_type=F32)
    marks[...] = local.reshape(requests, tree, LANES)
    depth[...] = (jnp.sum(local, axis=1, keepdims=True) - 1.0).reshape(requests, tree, 1)

    gather_pass(0)

    for r in range(requests):
        angles = (depth[r] + lengths[r].astype(F32)) * freq[...]
        turns[0, r] = jnp.cos(angles)
        turns[1, r] = jnp.sin(angles)

    for copy in loads:
        copy.wait()

    def reduce_copy(c, m):
        return pltpu.make_async_remote_copy(
            src_ref=outgoing.at[c, m],
            dst_ref=incoming.at[c, m],
            send_sem=rs_send.at[c, m],
            recv_sem=rs_recv.at[c, m],
            device_id=(req, flip(low(m))),
            device_id_type=MESH,
        )

    def reduce_sum(c, m):
        value = part[c, flip(m)].astype(F32)
        for b in strides:
            if m == 0 or b < low(m):
                reduce_copy(c, m | b).wait_recv()
                value += incoming[c, m | b].astype(F32)
        return value

    def reduce_start(c):
        for m in range(t - 1, 1, -2):
            outgoing[c, m] = part[c, flip(m)]
            reduce_copy(c, m).start()

    def reduce_pass(c):
        outgoing[c, 1] = part[c, flip(1)]
        reduce_copy(c, 1).start()
        for m in sorted(passed_on, key=low):
            outgoing[c, m] = reduce_sum(c, m).astype(BF16)
            reduce_copy(c, m).start()

    def chunk(c):
        gather_end(c)
        spread = jnp.zeros((crows, 1), F32)
        for g in range(t):
            value = full[c, g].astype(F32)
            spread += jnp.sum(value * value, axis=1, keepdims=True)
        inverse = lax.rsqrt(spread / (t * width) + 1e-05)
        for g in range(t):
            value = full[c, g].astype(F32)
            nrm[:, g * width : (g + 1) * width] = (value * inverse * gains[:, g * width : (g + 1) * width]).astype(BF16)
        normed = nrm[...]
        query = jnp.dot(normed, wq[...], preferred_element_type=F32)
        keyval = lax.dot_general(
            normed, wkv[...], (((1,), (1,)), ((), ())), preferred_element_type=F32
        )
        if c + 1 < chunks:
            gather_pass(c + 1)
        if c > 0:
            reduce_pass(c - 1)
        cosines = turns[0, c * per : (c + 1) * per].reshape(crows, HALF)
        sines = turns[1, c * per : (c + 1) * per].reshape(crows, HALF)

        def turn(value):
            first, second = value[:, :HALF], value[:, HALF:]
            return jnp.concatenate(
                [first * cosines - second * sines, second * cosines + first * sines], axis=1
            )

        for h in range(kv_local * GROUP):
            value = turn(query[:, h * HD : (h + 1) * HD]) * scale
            qs[h] = value.reshape(per, tree, HD)
        for i in range(2 * kv_local):
            value = keyval[:, i * HD : (i + 1) * HD]
            if i % 2 == 0:
                value = turn(value)
            value = value.astype(BF16).astype(F32).reshape(per, tree, HD)
            kvs[pl.ds(c * per, per), i] = value

        def attend(pair, inner):
            jobs = [(pair * TOGETHER + u, g) for u in range(TOGETHER) for g in range(kv_local)]
            scores = []
            for i, g in jobs:
                r = c * per + i
                q = qs[g * GROUP : (g + 1) * GROUP, i].reshape(GROUP * tree, HD).astype(BF16)
                tree_keys = jnp.concatenate([kvs[r, 2 * g], blank], axis=0).astype(BF16)
                keys = kept[r, g * 2 * HD : g * 2 * HD + HD, :]
                a = jnp.dot(q, keys, preferred_element_type=F32)
                b = lax.dot_general(
                    q, tree_keys, (((1,), (1,)), ((), ())), preferred_element_type=F32
                )
                scores.append((a, b))
            weights = []
            for (i, g), (a, b) in zip(jobs, scores):
                r = c * per + i
                mask = jnp.concatenate([marks[r]] * GROUP, axis=0) > 0.5
                both = jnp.concatenate(
                    [jnp.where(positions < lengths[r], a, -1e30), jnp.where(mask, b, -1e30)], axis=1
                )
                both = jnp.exp(both - jnp.max(both, axis=1, keepdims=True))
                weights.append((both.astype(BF16), jnp.sum(both, axis=1, keepdims=True)))
            results = []
            for (i, g), (both, total) in zip(jobs, weights):
                r = c * per + i
                values = kept[r, g * 2 * HD + HD : (g + 1) * 2 * HD, :]
                tree_values = jnp.concatenate([kvs[r, 2 * g + 1], blank], axis=0).astype(BF16)
                value = lax.dot_general(
                    both[:, :cache_len], values, (((1,), (1,)), ((), ())),
                    preferred_element_type=F32,
                ) + jnp.dot(both[:, cache_len:], tree_values, preferred_element_type=F32)
                results.append(value / total)
            for (i, g), value in zip(jobs, results):
                for j in range(GROUP):
                    h = g * GROUP + j
                    ctx[i, :, h * HD : (h + 1) * HD] = value[j * tree : (j + 1) * tree]
            return inner

        lax.fori_loop(0, per // TOGETHER, attend, 0)
        rounded = ctx[...].reshape(crows, kv_local * GROUP * HD).astype(BF16)
        for g in range(t):
            part[c, g] = jnp.dot(
                rounded, wo[:, g * width : (g + 1) * width], preferred_element_type=F32
            ).astype(BF16)

    blank = jnp.zeros((LANES - tree, HD), F32)
    for c in range(chunks):
        chunk(c)
        reduce_start(c)

    level_c = lax.broadcasted_iota(jnp.int32, (PAD, cache_len), 0)
    place_c = lax.broadcasted_iota(jnp.int32, (PAD, cache_len), 1)
    n_accept = accepted.shape[0]
    token = lax.broadcasted_iota(jnp.int32, (n_accept, tree), 1)
    asked = lax.broadcasted_iota(jnp.int32, accepted.shape, 1)

    def write_note(k, target):
        r = request_for(at_req(k))
        path = jnp.sum(jnp.where(asked == r, accepted[...], 0), axis=1, keepdims=True)
        pick = (token == path).astype(F32)
        pick = jnp.concatenate([pick, jnp.zeros((PAD - n_accept, tree), F32)], axis=0).astype(BF16)
        spot = jnp.logical_and(place_c == level_c + lengths[r], level_c < n_accept)
        target[k, 0:PAD, :] = spot.astype(F32).astype(BF16)
        chosen = [
            jnp.dot(pick, kvs[r, i].astype(BF16), preferred_element_type=F32)
            for i in range(2 * kv_local)
        ]
        chosen = jnp.concatenate(chosen, axis=1).astype(BF16)
        target[k, PAD : 2 * PAD, 0 : 2 * kv_local * HD] = chosen

    def note_copy(k):
        return pltpu.make_async_remote_copy(
            src_ref=note_out.at[k],
            dst_ref=note_in.at[k],
            send_sem=note_send.at[k],
            recv_sem=note_recv.at[k],
            device_id=(at_req(k), tp),
            device_id_type=MESH,
        )

    def send_note(k, carry):
        write_note(k, note_out)
        note_copy(k).start()
        return carry

    note_out[...] = jnp.zeros_like(note_out)
    lax.fori_loop(1, n, send_note, 0)
    note_in[0] = jnp.zeros_like(note_in[0])
    write_note(0, note_in)

    def out_copy(k):
        return pltpu.make_async_copy(
            landed.at[k], new_cache.at[lax.rem(req + n - k, n)], out_sem.at[k]
        )

    def finish(k):
        spot = note_in[k, 0:PAD, :]
        chosen = note_in[k, PAD : 2 * PAD, 0 : 2 * kv_local * HD]
        added = lax.dot_general(chosen, spot, (((0,), (0,)), ((), ())), preferred_element_type=F32)
        landed[k] = landed[k] + added.astype(BF16)
        out_copy(k).start()

    finish(0)
    reduce_pass(chunks - 1)

    def receive(k, carry):
        move_copy(k).wait_recv()
        note_copy(k).wait_recv()
        finish(k)
        return carry

    lax.fori_loop(1, n, receive, 0)

    for c in range(chunks):
        where = slice(c * crows, (c + 1) * crows)
        out_rows[where, :] = (reduce_sum(c, 0) + hidden[where, :].astype(F32)).astype(BF16)

    for c in range(chunks):
        for m in range(t):
            for b in strides:
                if m == 0 or b < low(m):
                    gather_copy(c, m, b).wait_send()
        for m in range(1, t):
            reduce_copy(c, m).wait_send()

    def drain(k, carry):
        move_copy(k).wait_send()
        note_copy(k).wait_send()
        out_copy(k).wait()
        return carry

    lax.fori_loop(1, n, drain, 0)
    out_copy(0).wait()


def hand_over(rows, cache, out_rows, new_cache, rows_held, held, in_sem, out_sem):
    count = cache.shape[0]
    moves = [(cache.at[i], held.at[i], new_cache.at[i]) for i in range(count)]
    moves.append((rows, rows_held, out_rows))
    first = [pltpu.make_async_copy(m[0], m[1], in_sem.at[i]) for i, m in enumerate(moves)]
    second = [pltpu.make_async_copy(m[1], m[2], out_sem.at[i]) for i, m in enumerate(moves)]
    for copy in first:
        copy.start()
    for copy, after in zip(first, second):
        copy.wait()
        after.start()
    for copy in second:
        copy.wait()


def per_device(
    n, t,
    hidden, norm_gain, w_query, w_keyval, w_out, kv_cache, lengths, parents, accepted, slot_of
):
    requests, tree, width = hidden.shape
    rows = requests * tree
    features = w_query.shape[0]
    q_width = w_query.shape[1]
    kv_rows = w_keyval.shape[0]
    cache_len = kv_cache.shape[2]
    chunks = 2
    per = requests // chunks
    crows = per * tree
    heads = q_width // HD
    freq = jnp.asarray(
        (10000.0 ** (-2.0 * np.arange(HALF, dtype=np.float64) / HD)).astype(np.float32)
    ).reshape(1, HALF)
    smem = pl.BlockSpec(memory_space=pltpu.SMEM)
    vmem = pl.BlockSpec(memory_space=pltpu.VMEM)
    hbm = pl.BlockSpec(memory_space=pl.ANY)
    dma = pltpu.SemaphoreType.DMA
    out_rows, new_cache = pl.pallas_call(
        functools.partial(kernel, n, t, chunks, requests, tree),
        out_shape=(
            jax.ShapeDtypeStruct((rows, width), BF16),
            jax.ShapeDtypeStruct(kv_cache.shape, BF16),
        ),
        in_specs=[smem] * 2 + [vmem] * 5 + [hbm] * 4,
        out_specs=(vmem, hbm),
        scratch_shapes=[
            pltpu.VMEM(w_query.shape, BF16),
            pltpu.VMEM(w_keyval.shape, BF16),
            pltpu.VMEM(w_out.shape, BF16),
            pltpu.VMEM(kv_cache.shape, BF16),
            pltpu.VMEM((n,) + kv_cache.shape[1:], BF16),
            pltpu.VMEM((n,) + kv_cache.shape[1:], BF16),
            pltpu.VMEM((n, 2 * PAD, cache_len), BF16),
            pltpu.VMEM((n, 2 * PAD, cache_len), BF16),
            pltpu.VMEM((chunks, t, crows, width), BF16),
            pltpu.VMEM((crows, features), BF16),
            pltpu.VMEM((heads, per, tree, HD), F32),
            pltpu.VMEM((requests, kv_rows // HD, tree, HD), F32),
            pltpu.VMEM((requests, tree, LANES), F32),
            pltpu.VMEM((requests, tree, 1), F32),
            pltpu.VMEM((per, tree, q_width), F32),
            pltpu.VMEM((chunks, t, crows, width), BF16),
            pltpu.VMEM((chunks, t, crows, width), BF16),
            pltpu.VMEM((chunks, t, crows, width), BF16),
            pltpu.VMEM((2, requests, tree, HALF), F32),
            dma((3,)),
            dma((requests,)),
            dma((chunks, t)),
            dma((chunks, t)),
            dma((chunks, t)),
            dma((chunks, t)),
            dma((n,)),
            dma((n,)),
            dma((n,)),
            dma((n,)),
            dma((n,)),
        ],
        compiler_params=pltpu.CompilerParams(
            collective_id=0, has_side_effects=True, vmem_limit_bytes=56 * 1024 * 1024
        ),
    )(
        lengths, slot_of, accepted.T, hidden.reshape(rows, width), norm_gain,
        freq, parents, w_query, w_keyval, w_out, kv_cache,
    )
    rows_shape, cache_shape = out_rows.shape, new_cache.shape
    out_rows, new_cache = pl.pallas_call(
        hand_over,
        out_shape=(
            jax.ShapeDtypeStruct(rows_shape, BF16),
            jax.ShapeDtypeStruct(cache_shape, BF16),
        ),
        in_specs=[hbm, hbm],
        out_specs=(hbm, hbm),
        scratch_shapes=[
            pltpu.VMEM(rows_shape, BF16),
            pltpu.VMEM(cache_shape, BF16),
            dma((cache_shape[0] + 1,)),
            dma((cache_shape[0] + 1,)),
        ],
        compiler_params=pltpu.CompilerParams(vmem_limit_bytes=60 * 1024 * 1024),
    )(out_rows, new_cache)
    return (out_rows.reshape(requests, tree, width), new_cache)


def solution(mesh):
    in_specs = (
        P("req", None, "tp"),
        P(),
        P(None, "tp"),
        P("tp", None),
        P("tp", None),
        P("req", "tp", None),
        P("req"),
        P("req", None),
        P("req", None),
        P("req"),
    )
    out_specs = (P("req", None, "tp"), P("req", "tp", None))
    return jax.shard_map(
        functools.partial(per_device, mesh.shape["req"], mesh.shape["tp"]),
        mesh=mesh, in_specs=in_specs, out_specs=out_specs, check_vma=False,
    )
```
